128 devices in a mesh: dp: 16 (over z_hi, x, core), tensor: 8 (over z_lo, y).
Axes of the slice: x: 4, y: 4, z: 4 (z_hi: 2, z_lo: 2; z = z_hi * 2 + z_lo), core: 2. Of those that a mesh axis runs over, the one named last changes fastest.
Arguments:
- teacher_states: bfloat16 [3, 2048, 2, 8192], P(None, 'dp', None, 'tensor'), may hold values from -8 to 8
- student_states: bfloat16 [3, 2048, 2, 3072], P(None, 'dp', None, 'tensor'), may hold values from -8 to 8
Outputs:
- relation_loss: float32 [], replicated
- student_grads: bfloat16 [3, 2048, 2, 3072], P(None, 'dp', None, 'tensor')
The draws below stay inside these ranges and needn't reach their ends.
All inputs are finite; a program needn't handle non-finite values.
Results may differ from the reference program's by a relative error of at most 0.0047.
Values may be sent and summed in bfloat16 or wider, within the bound.
A program may use at most 192 MiB of HBM per device.

```python
import math
import jax
import jax.numpy as jnp
from jax import lax

TD = 8192
SD = 3072
RH = 64
LENGTH = 2048
SEQS = 2


def head_spread(key):
    ranking = jnp.arange(RH, dtype=jnp.float32) / (RH - 1)
    jitter = jax.random.uniform(key, (RH,), jnp.float32, 0.85, 1.18)
    return 0.45 * jnp.sqrt(1.0 + ranking) * jitter


def token_scales(key, lower, upper):
    return jnp.exp(jax.random.uniform(key, (3, LENGTH, SEQS, 1, 1), jnp.float32, math.log(lower), math.log(upper)))


def draw_teacher_states(key, part):
    key = jax.random.fold_in(key, 11)
    key_head, key_body, key_row = jax.random.split(key, 3)
    head_width = TD // RH
    spread = head_spread(key_head)[None, None, None, :, None]
    shape = (3, LENGTH, SEQS, RH, head_width)
    states = jnp.clip(jax.random.normal(key_body, shape, jnp.float32), -4.0, 4.0)
    states = states * token_scales(key_row, 0.5, 1.5) * spread
    return states.reshape(3, LENGTH, SEQS, TD).astype(jnp.bfloat16)


def draw_student_states(key, part):
    key = jax.random.fold_in(key, 23)
    key_head, key_body, key_row = jax.random.split(key, 3)
    head_width = SD // RH
    spread = head_spread(key_head)[None, None, None, :, None]
    shape = (3, LENGTH, SEQS, RH, head_width)
    states = jnp.clip(jax.random.normal(key_body, shape, jnp.float32), -4.0, 4.0)
    states = states * token_scales(key_row, 0.5, 1.5) * spread
    return states.reshape(3, LENGTH, SEQS, SD).astype(jnp.bfloat16)


def setup_inputs(seed: int = 0) -> dict:
    key_list = jax.random.split(jax.random.key(seed), 3)
    return {
        "teacher_states": draw_teacher_states(jax.random.fold_in(key_list[2], 71), 0),
        "student_states": draw_student_states(jax.random.fold_in(key_list[2], 71), 0),
    }


loss_scale = 16.0


def pair_terms(pair_data):
    teacher_block, student_block = pair_data
    teacher_scale = 1.0 / (teacher_block.shape[1] ** 0.5)
    student_scale = 1.0 / (student_block.shape[1] ** 0.5)
    teacher_scores = jnp.dot(teacher_block, teacher_block.T, preferred_element_type=jnp.float32) * teacher_scale
    student_scores = jnp.dot(student_block, student_block.T, preferred_element_type=jnp.float32) * student_scale
    teacher_logs = teacher_scores - jax.nn.logsumexp(teacher_scores, axis=1, keepdims=True)
    student_logs = student_scores - jax.nn.logsumexp(student_scores, axis=1, keepdims=True)
    teacher_probs = jnp.exp(teacher_logs)
    kl_total = jnp.sum(teacher_probs * (teacher_logs - student_logs))
    score_grad = (loss_scale * (jnp.exp(student_logs) - teacher_probs)).astype(jnp.bfloat16)
    forward_part = jnp.dot(score_grad, student_block, preferred_element_type=jnp.float32)
    mirror_part = jnp.dot(score_grad.T, student_block, preferred_element_type=jnp.float32)
    block_grad = ((forward_part + mirror_part) * student_scale).astype(jnp.bfloat16)
    return block_grad, kl_total


def reference(teacher_states, student_states):
    grad_list = []
    kl_sum = jnp.zeros((), jnp.float32)
    for relation in range(3):
        teacher_pairs = teacher_states[relation].reshape(LENGTH, SEQS * RH, TD // RH).transpose(1, 0, 2)
        student_pairs = student_states[relation].reshape(LENGTH, SEQS * RH, SD // RH).transpose(1, 0, 2)
        pair_grads, pair_kl = lax.map(pair_terms, (teacher_pairs, student_pairs))
        grad_list.append(pair_grads.transpose(1, 0, 2).reshape(LENGTH, SEQS, SD))
        kl_sum = kl_sum + jnp.sum(pair_kl)
    relation_loss = kl_sum / (3 * SEQS * RH * LENGTH)
    return relation_loss, jnp.stack(grad_list)
```

```python
import functools
import math

import jax
import jax.numpy as jnp
from jax import lax
from jax.experimental import pallas as pl
from jax.experimental.pallas import tpu as pltpu
from jax.sharding import PartitionSpec as P

RELATIONS = 3
SEQS = 2
RH = 64
LENGTH = 2048
TW = 128
SW = 48
DP = 16
TENSOR = 8
ROWS = LENGTH // DP
HEADS = RH // TENSOR
BLOCK = 256
CHUNK = 256
LOSS_SCALE = 16.0
LOG2E = 1.0 / math.log(2.0)
T_SCALE = LOG2E / math.sqrt(TW)
S_SCALE = LOG2E / math.sqrt(SW)
MESH = pl.DeviceIdType.MESH
f32 = jnp.float32
bf16 = jnp.bfloat16


def dot_nt(a, b):
    return lax.dot_general(a, b, (((1,), (1,)), ((), ())), preferred_element_type=f32)


def dot_nn(a, b):
    return jnp.dot(a, b, preferred_element_type=f32)


def prepare(teacher, student, t_left, t_right, s_left, s_right, s_feat):
    norms = []
    largest = jnp.zeros((1, ROWS), f32)
    for p in range(DP):
        x = student[p].astype(f32)
        square = jnp.sum(x * x, axis=0, keepdims=True)
        norms.append(square)
        largest = jnp.maximum(largest, square)
    largest = jnp.max(largest, axis=1, keepdims=True)
    first = lax.broadcasted_iota(jnp.int32, (16, ROWS), 0) == 0
    ones = jnp.where(first, 1.0, 0.0)
    zeros = jnp.zeros((16, ROWS), f32)
    for p in range(DP):
        rows = slice(p * ROWS, (p + 1) * ROWS)
        x = student[p].astype(f32)
        scaled = x * S_SCALE
        high = scaled.astype(bf16)
        low = (scaled - high.astype(f32)).astype(bf16)
        shift = (0.5 * S_SCALE) * (jnp.sqrt(norms[p] * largest) + norms[p])
        shift = jnp.where(first, -shift, 0.0).astype(bf16)
        s_right[:, rows] = jnp.concatenate([high, low, shift, zeros.astype(bf16)], axis=0)
        s_left[rows, :] = jnp.concatenate([x, x, ones, zeros], axis=0).T.astype(bf16)
        s_feat[:, rows] = student[p]
        x = teacher[p]
        scaled = x.astype(f32) * T_SCALE
        high = scaled.astype(bf16)
        t_left[rows, 0:TW] = x
        t_left[rows, TW:] = x
        t_right[rows, 0:TW] = high
        t_right[rows, TW:] = (scaled - high.astype(f32)).astype(bf16)


def score_block(i, t_left, t_right, s_left, s_right, s_feat, t_exp, s_exp, total, kl):
    own = pl.ds(pl.multiple_of(i * BLOCK, BLOCK), BLOCK)
    t_own = t_right[own, :]
    s_own = s_right[:, own]
    count = LENGTH // CHUNK
    t_max, t_sum, cross = [], [], []
    s_sum = jnp.zeros((1, BLOCK), f32)
    for k in range(count):
        part = slice(k * CHUNK, (k + 1) * CHUNK)
        t = dot_nt(t_left[part, :], t_own)
        top = jnp.max(t, axis=0, keepdims=True)
        t = t - top
        s = dot_nn(s_left[part, :], s_own)
        te = jnp.exp2(t)
        se = jnp.exp2(s)
        t_max.append(top)
        t_sum.append(jnp.sum(te, axis=0, keepdims=True))
        cross.append(jnp.sum(te * (t - s), axis=0, keepdims=True))
        s_sum = s_sum + jnp.sum(se, axis=0, keepdims=True)
        t_exp[part, :] = te
        s_exp[part, :] = se
    top = functools.reduce(jnp.maximum, t_max)
    lift = [jnp.exp2(x - top) for x in t_max]
    z = sum(f * x for f, x in zip(lift, t_sum))
    cross = sum(f * (c + (m - top) * x) for f, c, m, x in zip(lift, cross, t_max, t_sum))
    kl[...] += math.log(2.0) * cross / z - jnp.log(z) + jnp.log(s_sum)
    s_gain = LOSS_SCALE / s_sum
    t_gain = LOSS_SCALE / z
    x_own = s_feat[:, own]
    forward = jnp.zeros((SW, BLOCK), f32)
    for k in range(count):
        part = slice(k * CHUNK, (k + 1) * CHUNK)
        grad = (s_exp[part, :] * s_gain - t_exp[part, :] * (t_gain * lift[k])).astype(bf16)
        forward = forward + dot_nn(s_feat[:, part], grad)
        total[:, part] += dot_nt(x_own, grad)
    total[:, own] += forward


def kernel(
    teacher_hbm, student_hbm, loss_out, grads_out,
    t_in, s_in, t_send, s_send, t_got, s_got, g_send, g_got,
    t_left, t_right, s_left, s_right, s_feat, t_exp, s_exp, total, kl,
    loss_a, loss_b,
    load_sem, t_send_sem, s_send_sem, g_send_sem, t_got_sem, s_got_sem, g_got_sem, loss_send_sem, loss_got_sem,
):
    me = lax.axis_index("dp")
    lane = lax.axis_index("tensor")

    def loads(r):
        return (
            pltpu.make_async_copy(teacher_hbm.at[r], t_in.at[r], load_sem.at[0, r]),
            pltpu.make_async_copy(student_hbm.at[r], s_in.at[r], load_sem.at[1, r]),
        )

    for r in range(RELATIONS):
        for copy in loads(r):
            copy.start()

    barrier = pltpu.get_barrier_semaphore()

    def greet_dp(n, carry):
        pl.semaphore_signal(barrier, inc=1, device_id={"dp": lax.rem(me + n, DP)}, device_id_type=MESH)
        return carry

    def greet_tensor(n, carry):
        pl.semaphore_signal(barrier, inc=1, device_id={"tensor": lax.rem(lane + n, TENSOR)}, device_id_type=MESH)
        return carry

    lax.fori_loop(1, DP, greet_dp, 0)
    lax.fori_loop(1, TENSOR, greet_tensor, 0)

    def pack(r):
        for copy in loads(r):
            copy.wait()
        for s in range(SEQS):
            x = s_in[r, :, s, :].astype(f32).T.astype(bf16)
            for a in range(HEADS):
                s_send[r, s * HEADS + a] = x[a * SW : (a + 1) * SW, :]
            x = t_in[r, :, s, :]
            for a in range(HEADS):
                t_send[r, s * HEADS + a] = x[:, a * TW : (a + 1) * TW]

    def send_blocks(source, target, send_sem, got_sem, r):
        def one(n, carry):
            to = lax.rem(me + n, DP)
            pltpu.make_async_remote_copy(
                src_ref=source.at[r, to],
                dst_ref=target.at[r, me],
                send_sem=send_sem.at[r],
                recv_sem=got_sem.at[r],
                device_id={"dp": to},
                device_id_type=MESH,
            ).start()
            return carry

        lax.fori_loop(1, DP, one, 0)
        target[r, me] = source[r, me]

    def wait_blocks(buffer, sem, r):
        span = buffer.at[r, pl.ds(0, DP - 1)]
        pltpu.make_async_copy(span, span, sem.at[r]).wait()

    def send_inputs(r):
        send_blocks(s_send, s_got, s_send_sem, s_got_sem, r)
        send_blocks(t_send, t_got, t_send_sem, t_got_sem, r)

    def place(r):
        wait_blocks(g_got, g_got_sem, r)
        for s in range(SEQS):
            x = g_got[r, s * HEADS : (s + 1) * HEADS].reshape(HEADS * SW, ROWS)
            grads_out[r, :, s, :] = x.T

    pack(0)
    pl.semaphore_wait(barrier, DP - 1 + TENSOR - 1)
    send_inputs(0)
    pack(1)
    pack(2)
    kl[...] = jnp.zeros_like(kl)

    def relation(r, carry):
        wait_blocks(s_got, s_got_sem, r)
        wait_blocks(t_got, t_got_sem, r)

        @pl.when(r < RELATIONS - 1)
        def _():
            send_inputs(r + 1)

        prepare(t_got.at[r], s_got.at[r], t_left, t_right, s_left, s_right, s_feat)
        total[...] = jnp.zeros_like(total)

        def step(i, inner):
            score_block(i, t_left, t_right, s_left, s_right, s_feat, t_exp, s_exp, total, kl)
            return inner

        lax.fori_loop(0, LENGTH // BLOCK, step, 0)
        for p in range(DP):
            g_send[r, p] = (total[:, p * ROWS : (p + 1) * ROWS] * (1.0 / math.sqrt(SW))).astype(bf16)
        send_blocks(g_send, g_got, g_send_sem, g_got_sem, r)

        @pl.when(r > 0)
        def _():
            place(r - 1)

        return carry

    lax.fori_loop(0, RELATIONS, relation, 0)

    def share(buffer, axis, here, size, which, value):
        buffer[here] = value

        def one(n, carry):
            to = lax.rem(here + n, size)
            pltpu.make_async_remote_copy(
                src_ref=buffer.at[here],
                dst_ref=buffer.at[here],
                send_sem=loss_send_sem.at[which],
                recv_sem=loss_got_sem.at[which],
                device_id={axis: to},
                device_id_type=MESH,
            ).start()
            return carry

        lax.fori_loop(1, size, one, 0)
        span = buffer.at[pl.ds(0, size - 1)]
        pltpu.make_async_copy(span, span, loss_got_sem.at[which]).wait()
        return functools.reduce(lambda a, b: a + b, [buffer[n] for n in range(size)])

    part = jnp.broadcast_to(jnp.sum(kl[...], axis=1, keepdims=True), (8, 128))
    part = share(loss_a, "dp", me, DP, 0, part)
    part = share(loss_b, "tensor", lane, TENSOR, 1, part)
    loss_out[...] = part * (1.0 / (RELATIONS * SEQS * RH * LENGTH))
    place(RELATIONS - 1)

    for r in range(RELATIONS):
        wait_blocks(t_send, t_send_sem, r)
        wait_blocks(s_send, s_send_sem, r)
        wait_blocks(g_send, g_send_sem, r)
    for which, buffer, size in ((0, loss_a, DP), (1, loss_b, TENSOR)):
        span = buffer.at[pl.ds(0, size - 1)]
        pltpu.make_async_copy(span, span, loss_send_sem.at[which]).wait()


def per_device(teacher_states, student_states):
    dma = pltpu.SemaphoreType.DMA
    loss, grads = pl.pallas_call(
        kernel,
        out_shape=(
            jax.ShapeDtypeStruct((8, 128), f32),
            jax.ShapeDtypeStruct(student_states.shape, bf16),
        ),
        in_specs=[pl.BlockSpec(memory_space=pl.ANY)] * 2,
        out_specs=(pl.BlockSpec(memory_space=pltpu.VMEM), pl.BlockSpec(memory_space=pltpu.VMEM)),
        scratch_shapes=[
            pltpu.VMEM((RELATIONS, ROWS, SEQS, HEADS * TW), bf16),
            pltpu.VMEM((RELATIONS, ROWS, SEQS, HEADS * SW), bf16),
            pltpu.VMEM((RELATIONS, DP, ROWS, TW), bf16),
            pltpu.VMEM((RELATIONS, DP, SW, ROWS), bf16),
            pltpu.VMEM((RELATIONS, DP, ROWS, TW), bf16),
            pltpu.VMEM((RELATIONS, DP, SW, ROWS), bf16),
            pltpu.VMEM((RELATIONS, DP, SW, ROWS), bf16),
            pltpu.VMEM((RELATIONS, DP, SW, ROWS), bf16),
            pltpu.VMEM((LENGTH, 2 * TW), bf16),
            pltpu.VMEM((LENGTH, 2 * TW), bf16),
            pltpu.VMEM((LENGTH, 128), bf16),
            pltpu.VMEM((128, LENGTH), bf16),
            pltpu.VMEM((SW, LENGTH), bf16),
            pltpu.VMEM((LENGTH, BLOCK), f32),
            pltpu.VMEM((LENGTH, BLOCK), f32),
            pltpu.VMEM((SW, LENGTH), f32),
            pltpu.VMEM((1, BLOCK), f32),
            pltpu.VMEM((DP, 8, 128), f32),
            pltpu.VMEM((TENSOR, 8, 128), f32),
            dma((2, RELATIONS)),
            dma((RELATIONS,)),
            dma((RELATIONS,)),
            dma((RELATIONS,)),
            dma((RELATIONS,)),
            dma((RELATIONS,)),
            dma((RELATIONS,)),
            dma((2,)),
            dma((2,)),
        ],
        compiler_params=pltpu.CompilerParams(
            collective_id=0, has_side_effects=True, vmem_limit_bytes=48 * 1024 * 1024
        ),
    )(teacher_states, student_states)
    return loss[0, 0], grads


def solution(mesh):
    placed = (P(None, "dp", None, "tensor"), P(None, "dp", None, "tensor"))
    return jax.shard_map(
        per_device,
        mesh=mesh,
        in_specs=placed,
        out_specs=(P(), P(None, "dp", None, "tensor")),
        check_vma=False,
    )
```

```python
import functools
import math

import jax
import jax.numpy as jnp
from jax import lax
from jax.experimental import pallas as pl
from jax.experimental.pallas import tpu as pltpu
from jax.sharding import PartitionSpec as P

RELATIONS = 3
SEQS = 2
RH = 64
LENGTH = 2048
TW = 128
SW = 48
DP = 16
TENSOR = 8
ROWS = LENGTH // DP
HEADS = RH // TENSOR
BLOCK = 256
CHUNK = 256
PIECE = 32
LOSS_SCALE = 16.0
LOG2E = 1.0 / math.log(2.0)
T_SCALE = LOG2E / math.sqrt(TW)
S_SCALE = LOG2E / math.sqrt(SW)
MESH = pl.DeviceIdType.MESH
f32 = jnp.float32
bf16 = jnp.bfloat16


def dot_nt(a, b):
    return lax.dot_general(a, b, (((1,), (1,)), ((), ())), preferred_element_type=f32)


def dot_nn(a, b):
    return jnp.dot(a, b, preferred_element_type=f32)


def prepare(teacher, student, t_left, t_right, s_left, s_right, s_feat):
    norms = []
    largest = jnp.zeros((1, ROWS), f32)
    for p in range(DP):
        x = student[p].astype(f32)
        square = jnp.sum(x * x, axis=0, keepdims=True)
        norms.append(square)
        largest = jnp.maximum(largest, square)
    largest = jnp.max(largest, axis=1, keepdims=True)
    first = lax.broadcasted_iota(jnp.int32, (16, ROWS), 0) == 0
    ones = jnp.where(first, 1.0, 0.0)
    zeros = jnp.zeros((16, ROWS), f32)
    for p in range(DP):
        rows = slice(p * ROWS, (p + 1) * ROWS)
        x = student[p].astype(f32)
        scaled = x * S_SCALE
        high = scaled.astype(bf16)
        low = (scaled - high.astype(f32)).astype(bf16)
        shift = (0.5 * S_SCALE) * (jnp.sqrt(norms[p] * largest) + norms[p])
        shift = jnp.where(first, -shift, 0.0).astype(bf16)
        s_right[:, rows] = jnp.concatenate([high, low, shift, zeros.astype(bf16)], axis=0)
        s_left[rows, :] = jnp.concatenate([x, x, ones, zeros], axis=0).T.astype(bf16)
        s_feat[:, rows] = student[p]
        x = teacher[p]
        scaled = x.astype(f32) * T_SCALE
        high = scaled.astype(bf16)
        t_left[rows, 0:TW] = x
        t_left[rows, TW:] = x
        t_right[rows, 0:TW] = high
        t_right[rows, TW:] = (scaled - high.astype(f32)).astype(bf16)


def fold(x, op):
    parts = [x[8 * n : 8 * n + 8, :] for n in range(x.shape[0] // 8)]
    while len(parts) > 1:
        parts = [op(*parts[n : n + 2]) if n + 1 < len(parts) else parts[n] for n in range(0, len(parts), 2)]
    return parts[0]


def score_step(i, now, before, t_left, t_right, s_left, s_right, s_feat, t_exp, s_exp, gain, total, kl):
    count = LENGTH // CHUNK
    repeat = PIECE // 8
    if before:
        last = pl.ds(pl.multiple_of((i - 1) * BLOCK, BLOCK), BLOCK)
        x_last = s_feat[:, last]
        s_gain = jnp.concatenate([gain[count * 8 :, :]] * repeat, axis=0)
        t_gain = [gain[k * 8 : k * 8 + 8, :] for k in range(count)]
        forward = jnp.zeros((SW, BLOCK), f32)
    if now:
        own = pl.ds(pl.multiple_of(i * BLOCK, BLOCK), BLOCK)
        t_own = t_right[own, :]
        s_own = s_right[:, own]
        t_max, t_sum, cross = [], [], []
        s_sum = jnp.zeros((8, BLOCK), f32)
    for k in range(count):
        part = slice(k * CHUNK, (k + 1) * CHUNK)
        pieces = [slice(n, n + PIECE) for n in range(k * CHUNK, (k + 1) * CHUNK, PIECE)]
        if before:
            t_wide = jnp.concatenate([t_gain[k]] * repeat, axis=0)
            grad = jnp.concatenate(
                [(s_exp[n, :] * s_gain - t_exp[n, :] * t_wide).astype(bf16) for n in pieces], axis=0
            )
            forward = forward + dot_nn(s_feat[:, part], grad)
            total[:, part] += dot_nt(x_last, grad)
        if now:
            t_all = dot_nt(t_left[part, :], t_own)
            s_all = dot_nn(s_left[part, :], s_own)
            top = fold(t_all, jnp.maximum)
            top_wide = jnp.concatenate([top] * repeat, axis=0)
            z = jnp.zeros((8, BLOCK), f32)
            c = jnp.zeros((8, BLOCK), f32)
            for m, n in enumerate(pieces):
                t = t_all[m * PIECE : (m + 1) * PIECE, :] - top_wide
                s = s_all[m * PIECE : (m + 1) * PIECE, :]
                te = jnp.exp2(t)
                se = jnp.exp2(s)
                z = z + fold(te, jnp.add)
                s_sum = s_sum + fold(se, jnp.add)
                c = c + fold(te * (t - s), jnp.add)
                t_exp[n, :] = te
                s_exp[n, :] = se
            t_max.append(top)
            t_sum.append(z)
            cross.append(c)
    if before:
        total[:, last] += forward
    if now:
        top = functools.reduce(jnp.maximum, t_max)
        top = jnp.broadcast_to(jnp.max(top, axis=0, keepdims=True), (8, BLOCK))
        lift = [jnp.exp2(x - top) for x in t_max]
        z = sum(f * x for f, x in zip(lift, t_sum))
        c = sum(f * (c + (m - top) * x) for f, c, m, x in zip(lift, cross, t_max, t_sum))
        z = jnp.sum(z, axis=0, keepdims=True)
        c = jnp.sum(c, axis=0, keepdims=True)
        s_sum = jnp.sum(s_sum, axis=0, keepdims=True)
        kl[...] += math.log(2.0) * c / z - jnp.log(z) + jnp.log(s_sum)
        t_gain = jnp.broadcast_to(LOSS_SCALE / z, (8, BLOCK))
        for k in range(count):
            gain[k * 8 : k * 8 + 8, :] = t_gain * lift[k]
        gain[count * 8 :, :] = jnp.broadcast_to(LOSS_SCALE / s_sum, (8, BLOCK))


def kernel(
    teacher_hbm, student_hbm, loss_out, grads_out,
    t_in, s_in, t_send, s_send, t_got, s_got, g_send, g_got,
    t_left, t_right, s_left, s_right, s_feat, t_exp, s_exp, gain, total, kl,
    loss_a, loss_b,
    load_sem, t_send_sem, s_send_sem, g_send_sem, t_got_sem, s_got_sem, g_got_sem, loss_send_sem, loss_got_sem,
):
    me = lax.axis_index("dp")
    lane = lax.axis_index("tensor")

    def loads(r):
        return (
            pltpu.make_async_copy(teacher_hbm.at[r], t_in.at[r], load_sem.at[0, r]),
            pltpu.make_async_copy(student_hbm.at[r], s_in.at[r], load_sem.at[1, r]),
        )

    for r in range(RELATIONS):
        for copy in loads(r):
            copy.start()

    barrier = pltpu.get_barrier_semaphore()

    def greet_dp(n, carry):
        pl.semaphore_signal(barrier, inc=1, device_id={"dp": lax.rem(me + n, DP)}, device_id_type=MESH)
        return carry

    def greet_tensor(n, carry):
        pl.semaphore_signal(barrier, inc=1, device_id={"tensor": lax.rem(lane + n, TENSOR)}, device_id_type=MESH)
        return carry

    lax.fori_loop(1, DP, greet_dp, 0)
    lax.fori_loop(1, TENSOR, greet_tensor, 0)

    def pack(r):
        for copy in loads(r):
            copy.wait()
        for s in range(SEQS):
            x = s_in[r, :, s, :].astype(f32).T.astype(bf16)
            for a in range(HEADS):
                s_send[r, s * HEADS + a] = x[a * SW : (a + 1) * SW, :]
            x = t_in[r, :, s, :]
            for a in range(HEADS):
                t_send[r, s * HEADS + a] = x[:, a * TW : (a + 1) * TW]

    def send_blocks(source, target, send_sem, got_sem, r):
        def one(n, carry):
            to = lax.rem(me + n, DP)
            pltpu.make_async_remote_copy(
                src_ref=source.at[r, to],
                dst_ref=target.at[r, me],
                send_sem=send_sem.at[r],
                recv_sem=got_sem.at[r],
                device_id={"dp": to},
                device_id_type=MESH,
            ).start()
            return carry

        lax.fori_loop(1, DP, one, 0)
        target[r, me] = source[r, me]

    def wait_blocks(buffer, sem, r):
        span = buffer.at[r, pl.ds(0, DP - 1)]
        pltpu.make_async_copy(span, span, sem.at[r]).wait()

    def send_inputs(r):
        send_blocks(s_send, s_got, s_send_sem, s_got_sem, r)
        send_blocks(t_send, t_got, t_send_sem, t_got_sem, r)

    def place(r):
        wait_blocks(g_got, g_got_sem, r)
        for s in range(SEQS):
            x = g_got[r, s * HEADS : (s + 1) * HEADS].reshape(HEADS * SW, ROWS)
            grads_out[r, :, s, :] = x.T

    pack(0)
    pl.semaphore_wait(barrier, DP - 1 + TENSOR - 1)
    send_inputs(0)
    pack(1)
    pack(2)
    kl[...] = jnp.zeros_like(kl)

    def relation(r, carry):
        wait_blocks(s_got, s_got_sem, r)
        wait_blocks(t_got, t_got_sem, r)

        @pl.when(r == 0)
        def _():
            for n in range(1, RELATIONS):
                send_inputs(n)

        prepare(t_got.at[r], s_got.at[r], t_left, t_right, s_left, s_right, s_feat)
        total[...] = jnp.zeros_like(total)

        refs = (t_left, t_right, s_left, s_right, s_feat, t_exp, s_exp, gain, total, kl)

        def step(i, inner):
            score_step(i, True, True, *refs)
            return inner

        score_step(0, True, False, *refs)
        lax.fori_loop(1, LENGTH // BLOCK, step, 0)
        score_step(LENGTH // BLOCK, False, True, *refs)
        for p in range(DP):
            g_send[r, p] = (total[:, p * ROWS : (p + 1) * ROWS] * (1.0 / math.sqrt(SW))).astype(bf16)
        send_blocks(g_send, g_got, g_send_sem, g_got_sem, r)

        @pl.when(r > 0)
        def _():
            place(r - 1)

        return carry

    lax.fori_loop(0, RELATIONS, relation, 0)

    def share(buffer, axis, here, size, which, value):
        buffer[here] = value

        def one(n, carry):
            to = lax.rem(here + n, size)
            pltpu.make_async_remote_copy(
                src_ref=buffer.at[here],
                dst_ref=buffer.at[here],
                send_sem=loss_send_sem.at[which],
                recv_sem=loss_got_sem.at[which],
                device_id={axis: to},
                device_id_type=MESH,
            ).start()
            return carry

        lax.fori_loop(1, size, one, 0)
        span = buffer.at[pl.ds(0, size - 1)]
        pltpu.make_async_copy(span, span, loss_got_sem.at[which]).wait()
        return functools.reduce(lambda a, b: a + b, [buffer[n] for n in range(size)])

    part = jnp.broadcast_to(jnp.sum(kl[...], axis=1, keepdims=True), (8, 128))
    part = share(loss_a, "dp", me, DP, 0, part)
    part = share(loss_b, "tensor", lane, TENSOR, 1, part)
    loss_out[...] = part * (1.0 / (RELATIONS * SEQS * RH * LENGTH))
    place(RELATIONS - 1)

    for r in range(RELATIONS):
        wait_blocks(t_send, t_send_sem, r)
        wait_blocks(s_send, s_send_sem, r)
        wait_blocks(g_send, g_send_sem, r)
    for which, buffer, size in ((0, loss_a, DP), (1, loss_b, TENSOR)):
        span = buffer.at[pl.ds(0, size - 1)]
        pltpu.make_async_copy(span, span, loss_send_sem.at[which]).wait()


def per_device(teacher_states, student_states):
    dma = pltpu.SemaphoreType.DMA
    loss, grads = pl.pallas_call(
        kernel,
        out_shape=(
            jax.ShapeDtypeStruct((8, 128), f32),
            jax.ShapeDtypeStruct(student_states.shape, bf16),
        ),
        in_specs=[pl.BlockSpec(memory_space=pl.ANY)] * 2,
        out_specs=(pl.BlockSpec(memory_space=pltpu.VMEM), pl.BlockSpec(memory_space=pltpu.VMEM)),
        scratch_shapes=[
            pltpu.VMEM((RELATIONS, ROWS, SEQS, HEADS * TW), bf16),
            pltpu.VMEM((RELATIONS, ROWS, SEQS, HEADS * SW), bf16),
            pltpu.VMEM((RELATIONS, DP, ROWS, TW), bf16),
            pltpu.VMEM((RELATIONS, DP, SW, ROWS), bf16),
            pltpu.VMEM((RELATIONS, DP, ROWS, TW), bf16),
            pltpu.VMEM((RELATIONS, DP, SW, ROWS), bf16),
            pltpu.VMEM((RELATIONS, DP, SW, ROWS), bf16),
            pltpu.VMEM((RELATIONS, DP, SW, ROWS), bf16),
            pltpu.VMEM((LENGTH, 2 * TW), bf16),
            pltpu.VMEM((LENGTH, 2 * TW), bf16),
            pltpu.VMEM((LENGTH, 128), bf16),
            pltpu.VMEM((128, LENGTH), bf16),
            pltpu.VMEM((SW, LENGTH), bf16),
            pltpu.VMEM((LENGTH, BLOCK), f32),
            pltpu.VMEM((LENGTH, BLOCK), f32),
            pltpu.VMEM((8 * (LENGTH // CHUNK + 1), BLOCK), f32),
            pltpu.VMEM((SW, LENGTH), f32),
            pltpu.VMEM((1, BLOCK), f32),
            pltpu.VMEM((DP, 8, 128), f32),
            pltpu.VMEM((TENSOR, 8, 128), f32),
            dma((2, RELATIONS)),
            dma((RELATIONS,)),
            dma((RELATIONS,)),
            dma((RELATIONS,)),
            dma((RELATIONS,)),
            dma((RELATIONS,)),
            dma((RELATIONS,)),
            dma((2,)),
            dma((2,)),
        ],
        compiler_params=pltpu.CompilerParams(
            collective_id=0, has_side_effects=True, vmem_limit_bytes=62 * 1024 * 1024
        ),
    )(teacher_states, student_states)
    return loss[0, 0], grads


def solution(mesh):
    placed = (P(None, "dp", None, "tensor"), P(None, "dp", None, "tensor"))
    return jax.shard_map(
        per_device,
        mesh=mesh,
        in_specs=placed,
        out_specs=(P(), P(None, "dp", None, "tensor")),
        check_vma=False,
    )
```

```python
import functools
import math

import jax
import jax.numpy as jnp
from jax import lax
from jax.experimental import pallas as pl
from jax.experimental.pallas import tpu as pltpu
from jax.sharding import PartitionSpec as P

RELATIONS = 3
SEQS = 2
RH = 64
LENGTH = 2048
TW = 128
SW = 48
DP = 16
TENSOR = 8
ROWS = LENGTH // DP
HEADS = RH // TENSOR
BLOCK = 256
BLOCKS = LENGTH // BLOCK
CHUNK = 512
COUNT = LENGTH // CHUNK
PIECE = 32
LOSS_SCALE = 16.0
LOG2E = 1.0 / math.log(2.0)
T_SCALE = LOG2E / math.sqrt(TW)
S_SCALE = LOG2E / math.sqrt(SW)
MESH = pl.DeviceIdType.MESH
f32 = jnp.float32
bf16 = jnp.bfloat16


def dot_nt(a, b):
    return lax.dot_general(a, b, (((1,), (1,)), ((), ())), preferred_element_type=f32)


def dot_nn(a, b):
    return jnp.dot(a, b, preferred_element_type=f32)


def prepare(blocks, t_left, t_right, s_left, s_right, s_feat):
    norms = []
    largest = jnp.zeros((1, ROWS), f32)
    for p in range(DP):
        x = blocks[p, 0:SW, :].astype(f32)
        square = jnp.sum(x * x, axis=0, keepdims=True)
        norms.append(square)
        largest = jnp.maximum(largest, square)
    largest = jnp.max(largest, axis=1, keepdims=True)
    first = lax.broadcasted_iota(jnp.int32, (16, ROWS), 0) == 0
    ones = jnp.where(first, 1.0, 0.0)
    zeros = jnp.zeros((16, ROWS), f32)
    for p in range(DP):
        rows = slice(p * ROWS, (p + 1) * ROWS)
        features = blocks[p, 0:SW, :]
        x = features.astype(f32)
        scaled = x * S_SCALE
        high = scaled.astype(bf16)
        low = (scaled - high.astype(f32)).astype(bf16)
        shift = (0.5 * S_SCALE) * (jnp.sqrt(norms[p] * largest) + norms[p])
        shift = jnp.where(first, -shift, 0.0).astype(bf16)
        s_right[:, rows] = jnp.concatenate([high, low, shift, zeros.astype(bf16)], axis=0)
        s_left[rows, :] = jnp.concatenate([x, x, ones, zeros], axis=0).T.astype(bf16)
        s_feat[:, rows] = features
        x = blocks[p, SW:, :]
        scaled = x.astype(f32) * T_SCALE
        high = scaled.astype(bf16)
        t_left[rows, 0:TW] = x
        t_left[rows, TW:] = x
        t_right[rows, 0:TW] = high
        t_right[rows, TW:] = (scaled - high.astype(f32)).astype(bf16)


def fold(x, op):
    parts = [x[8 * n : 8 * n + 8, :] for n in range(x.shape[0] // 8)]
    while len(parts) > 1:
        parts = [op(*parts[n : n + 2]) if n + 1 < len(parts) else parts[n] for n in range(0, len(parts), 2)]
    return parts[0]


def pipeline_step(scores, exps, grads, work):
    t_raw, s_raw, t_exp, s_exp, t_top, gain, kl = work
    repeat = PIECE // 8
    if grads is not None:
        (s_feat, total), block = grads
        last = pl.ds(pl.multiple_of(block * BLOCK, BLOCK), BLOCK)
        x_last = s_feat[:, last]
        s_gain = jnp.concatenate([gain[COUNT * 8 :, :]] * repeat, axis=0)
        t_gain = [gain[k * 8 : k * 8 + 8, :] for k in range(COUNT)]
        forward = jnp.zeros((SW, BLOCK), f32)
    if exps:
        t_max = [t_top[k * 8 : k * 8 + 8, :] for k in range(COUNT)]
        t_sum, cross = [], []
        s_sum = jnp.zeros((8, BLOCK), f32)
    if scores is not None:
        (t_left, t_right, s_left, s_right), block = scores
        own = pl.ds(pl.multiple_of(block * BLOCK, BLOCK), BLOCK)
        t_own = t_right[own, :]
        s_own = s_right[:, own]
    for k in range(COUNT):
        part = slice(k * CHUNK, (k + 1) * CHUNK)
        pieces = [slice(n, n + PIECE) for n in range(k * CHUNK, (k + 1) * CHUNK, PIECE)]
        if grads is not None:
            t_wide = jnp.concatenate([t_gain[k]] * repeat, axis=0)
            grad = jnp.concatenate(
                [(s_exp[n, :] * s_gain - t_exp[n, :] * t_wide).astype(bf16) for n in pieces], axis=0
            )
            forward = forward + dot_nn(s_feat[:, part], grad)
            total[:, part] += dot_nt(x_last, grad)
        if exps:
            top_wide = jnp.concatenate([t_max[k]] * repeat, axis=0)
            z = jnp.zeros((8, BLOCK), f32)
            c = jnp.zeros((8, BLOCK), f32)
            for n in pieces:
                t = t_raw[n, :] - top_wide
                s = s_raw[n, :]
                te = jnp.exp2(t)
                se = jnp.exp2(s)
                z = z + fold(te, jnp.add)
                s_sum = s_sum + fold(se, jnp.add)
                c = c + fold(te * (t - s), jnp.add)
                t_exp[n, :] = te
                s_exp[n, :] = se
            t_sum.append(z)
            cross.append(c)
        if scores is not None:
            t_all = dot_nt(t_left[part, :], t_own)
            t_raw[part, :] = t_all
            t_top[k * 8 : k * 8 + 8, :] = fold(t_all, jnp.maximum)
            s_raw[part, :] = dot_nn(s_left[part, :], s_own)
    if grads is not None:
        total[:, last] += forward
    if exps:
        top = functools.reduce(jnp.maximum, t_max)
        top = jnp.broadcast_to(jnp.max(top, axis=0, keepdims=True), (8, BLOCK))
        lift = [jnp.exp2(x - top) for x in t_max]
        z = sum(f * x for f, x in zip(lift, t_sum))
        c = sum(f * (c + (m - top) * x) for f, c, m, x in zip(lift, cross, t_max, t_sum))
        z = jnp.sum(z, axis=0, keepdims=True)
        c = jnp.sum(c, axis=0, keepdims=True)
        s_sum = jnp.sum(s_sum, axis=0, keepdims=True)
        kl[...] += math.log(2.0) * c / z - jnp.log(z) + jnp.log(s_sum)
        t_gain = jnp.broadcast_to(LOSS_SCALE / z, (8, BLOCK))
        for k in range(COUNT):
            gain[k * 8 : k * 8 + 8, :] = t_gain * lift[k]
        gain[COUNT * 8 :, :] = jnp.broadcast_to(LOSS_SCALE / s_sum, (8, BLOCK))


def kernel(
    teacher_hbm, student_hbm, loss_out, grads_out,
    t_in, s_in, send, got, g_send, g_got,
    t_left, t_right, s_left, s_right, s_feat, total,
    t_raw, s_raw, t_exp, s_exp, t_top, gain, kl,
    loss_a, loss_b,
    load_sem, send_sem, got_sem, g_send_sem, g_got_sem, loss_send_sem, loss_got_sem,
):
    me = lax.axis_index("dp")
    lane = lax.axis_index("tensor")

    def loads(r):
        return (
            pltpu.make_async_copy(student_hbm.at[r], s_in.at[r], load_sem.at[1, r]),
            pltpu.make_async_copy(teacher_hbm.at[r], t_in.at[r], load_sem.at[0, r]),
        )

    for r in range(RELATIONS):
        for copy in loads(r):
            copy.start()

    barrier = pltpu.get_barrier_semaphore()

    def greet_dp(n, carry):
        pl.semaphore_signal(barrier, inc=1, device_id={"dp": lax.rem(me + n, DP)}, device_id_type=MESH)
        return carry

    def greet_tensor(n, carry):
        pl.semaphore_signal(barrier, inc=1, device_id={"tensor": lax.rem(lane + n, TENSOR)}, device_id_type=MESH)
        return carry

    lax.fori_loop(1, DP, greet_dp, 0)
    lax.fori_loop(1, TENSOR, greet_tensor, 0)

    def pack(r):
        student, teacher = loads(r)
        student.wait()
        for s in range(SEQS):
            x = s_in[r, :, s, :].astype(f32).T.astype(bf16)
            for a in range(HEADS):
                send[r, s * HEADS + a, 0:SW, :] = x[a * SW : (a + 1) * SW, :]
        teacher.wait()
        for s in range(SEQS):
            x = t_in[r, :, s, :]
            for a in range(HEADS):
                send[r, s * HEADS + a, SW:, :] = x[:, a * TW : (a + 1) * TW]

    def send_blocks(source, target, source_sem, target_sem, r):
        def one(n, carry):
            to = lax.rem(me + n, DP)
            pltpu.make_async_remote_copy(
                src_ref=source.at[r, to],
                dst_ref=target.at[r, me],
                send_sem=source_sem.at[r],
                recv_sem=target_sem.at[r],
                device_id={"dp": to},
                device_id_type=MESH,
            ).start()
            return carry

        lax.fori_loop(1, DP, one, 0)
        target[r, me] = source[r, me]

    def wait_blocks(buffer, sem, r):
        span = buffer.at[r, pl.ds(0, DP - 1)]
        pltpu.make_async_copy(span, span, sem.at[r]).wait()

    def place(r):
        wait_blocks(g_got, g_got_sem, r)
        for s in range(SEQS):
            x = g_got[r, s * HEADS : (s + 1) * HEADS].reshape(HEADS * SW, ROWS)
            grads_out[r, :, s, :] = x.T

    def receive(r):
        wait_blocks(got, got_sem, r)
        half = lax.rem(r, 2)
        prepare(got.at[r], t_left.at[half], t_right.at[half], s_left.at[half], s_right.at[half], s_feat.at[half])

    def give_back(r):
        half = lax.rem(r, 2)
        for p in range(DP):
            g_send[r, p] = (total[half, :, p * ROWS : (p + 1) * ROWS] * (1.0 / math.sqrt(SW))).astype(bf16)
        send_blocks(g_send, g_got, g_send_sem, g_got_sem, r)

    def for_scores(n):
        half = lax.rem(n // BLOCKS, 2)
        return (t_left.at[half], t_right.at[half], s_left.at[half], s_right.at[half]), lax.rem(n, BLOCKS)

    def for_grads(n):
        half = lax.rem(n // BLOCKS, 2)
        return (s_feat.at[half], total.at[half]), lax.rem(n, BLOCKS)

    work = (t_raw, s_raw, t_exp, s_exp, t_top, gain, kl)

    pack(0)
    pl.semaphore_wait(barrier, DP - 1 + TENSOR - 1)
    send_blocks(send, got, send_sem, got_sem, 0)
    pack(1)
    pack(2)
    kl[...] = jnp.zeros_like(kl)
    gain[...] = jnp.zeros_like(gain)
    t_exp[...] = jnp.zeros_like(t_exp)
    s_exp[...] = jnp.zeros_like(s_exp)
    s_feat[1] = jnp.zeros_like(s_feat[1])
    total[...] = jnp.zeros_like(total)
    send_blocks(send, got, send_sem, got_sem, 1)
    receive(0)
    pipeline_step(for_scores(0), False, None, work)

    def step(n, carry):
        block = lax.rem(n, BLOCKS)
        r = n // BLOCKS

        @pl.when(n == 0)
        def _():
            send_blocks(send, got, send_sem, got_sem, 2)

        @pl.when((block == BLOCKS - 1) & (r < RELATIONS - 1))
        def _():
            receive(r + 1)

        pipeline_step(for_scores(n + 1), True, for_grads(n + 2 * BLOCKS - 1), work)

        @pl.when((block == 0) & (r > 0))
        def _():
            give_back(r - 1)

        @pl.when((block == 0) & (r < RELATIONS - 1))
        def _():
            half = lax.rem(r + 1, 2)
            total[half] = jnp.zeros((SW, LENGTH), f32)

        return carry

    lax.fori_loop(0, RELATIONS * BLOCKS, step, 0)

    def share(buffer, axis, here, size, which, value):
        buffer[here] = value

        def one(n, carry):
            to = lax.rem(here + n, size)
            pltpu.make_async_remote_copy(
                src_ref=buffer.at[here],
                dst_ref=buffer.at[here],
                send_sem=loss_send_sem.at[which],
                recv_sem=loss_got_sem.at[which],
                device_id={axis: to},
                device_id_type=MESH,
            ).start()
            return carry

        lax.fori_loop(1, size, one, 0)

    def collect(buffer, size, which):
        span = buffer.at[pl.ds(0, size - 1)]
        pltpu.make_async_copy(span, span, loss_got_sem.at[which]).wait()
        return functools.reduce(lambda a, b: a + b, [buffer[n] for n in range(size)])

    part = jnp.broadcast_to(jnp.sum(kl[...], axis=1, keepdims=True), (8, 128))
    share(loss_a, "dp", me, DP, 0, part)
    pipeline_step(None, False, for_grads(RELATIONS * BLOCKS - 1), work)
    give_back(RELATIONS - 1)
    share(loss_b, "tensor", lane, TENSOR, 1, collect(loss_a, DP, 0))
    for r in range(RELATIONS - 1):
        place(r)
    loss_out[...] = collect(loss_b, TENSOR, 1) * (1.0 / (RELATIONS * SEQS * RH * LENGTH))
    for r in range(RELATIONS):
        wait_blocks(send, send_sem, r)
        wait_blocks(g_send, g_send_sem, r)
    for which, buffer, size in ((0, loss_a, DP), (1, loss_b, TENSOR)):
        span = buffer.at[pl.ds(0, size - 1)]
        pltpu.make_async_copy(span, span, loss_send_sem.at[which]).wait()
    place(RELATIONS - 1)


def per_device(teacher_states, student_states):
    dma = pltpu.SemaphoreType.DMA
    loss, grads = pl.pallas_call(
        kernel,
        out_shape=(
            jax.ShapeDtypeStruct((8, 128), f32),
            jax.ShapeDtypeStruct(student_states.shape, bf16),
        ),
        in_specs=[pl.BlockSpec(memory_space=pl.ANY)] * 2,
        out_specs=(pl.BlockSpec(memory_space=pltpu.VMEM), pl.BlockSpec(memory_space=pltpu.VMEM)),
        scratch_shapes=[
            pltpu.VMEM((RELATIONS, ROWS, SEQS, HEADS * TW), bf16),
            pltpu.VMEM((RELATIONS, ROWS, SEQS, HEADS * SW), bf16),
            pltpu.VMEM((RELATIONS, DP, SW + ROWS, 128), bf16),
            pltpu.VMEM((RELATIONS, DP, SW + ROWS, 128), bf16),
            pltpu.VMEM((RELATIONS, DP, SW, ROWS), bf16),
            pltpu.VMEM((RELATIONS, DP, SW, ROWS), bf16),
            pltpu.VMEM((2, LENGTH, 2 * TW), bf16),
            pltpu.VMEM((2, LENGTH, 2 * TW), bf16),
            pltpu.VMEM((2, LENGTH, 128), bf16),
            pltpu.VMEM((2, 128, LENGTH), bf16),
            pltpu.VMEM((2, SW, LENGTH), bf16),
            pltpu.VMEM((2, SW, LENGTH), f32),
            pltpu.VMEM((LENGTH, BLOCK), f32),
            pltpu.VMEM((LENGTH, BLOCK), f32),
            pltpu.VMEM((LENGTH, BLOCK), f32),
            pltpu.VMEM((LENGTH, BLOCK), f32),
            pltpu.VMEM((8 * COUNT, BLOCK), f32),
            pltpu.VMEM((8 * (COUNT + 1), BLOCK), f32),
            pltpu.VMEM((1, BLOCK), f32),
            pltpu.VMEM((DP, 8, 128), f32),
            pltpu.VMEM((TENSOR, 8, 128), f32),
            dma((2, RELATIONS)),
            dma((RELATIONS,)),
            dma((RELATIONS,)),
            dma((RELATIONS,)),
            dma((RELATIONS,)),
            dma((2,)),
            dma((2,)),
        ],
        compiler_params=pltpu.CompilerParams(
            collective_id=0, has_side_effects=True, vmem_limit_bytes=54000 * 1024
        ),
    )(teacher_states, student_states)
    return loss[0, 0], grads


def solution(mesh):
    placed = (P(None, "dp", None, "tensor"), P(None, "dp", None, "tensor"))
    return jax.shard_map(
        per_device,
        mesh=mesh,
        in_specs=placed,
        out_specs=(P(), P(None, "dp", None, "tensor")),
        check_vma=False,
    )
```

```python
import functools
import math

import jax
import jax.numpy as jnp
from jax import lax
from jax.experimental import pallas as pl
from jax.experimental.pallas import tpu as pltpu
from jax.sharding import PartitionSpec as P

RELATIONS = 3
SEQS = 2
RH = 64
LENGTH = 2048
TW = 128
SW = 48
DP = 16
TENSOR = 8
ROWS = LENGTH // DP
HEADS = RH // TENSOR
BLOCK = 256
BLOCKS = LENGTH // BLOCK
CHUNK = 512
COUNT = LENGTH // CHUNK
PIECE = 32
LOSS_SCALE = 16.0
LOG2E = 1.0 / math.log(2.0)
T_SCALE = LOG2E / math.sqrt(TW)
S_SCALE = LOG2E / math.sqrt(SW)
MESH = pl.DeviceIdType.MESH
f32 = jnp.float32
bf16 = jnp.bfloat16


def dot_nt(a, b):
    return lax.dot_general(a, b, (((1,), (1,)), ((), ())), preferred_element_type=f32)


def dot_nn(a, b):
    return jnp.dot(a, b, preferred_element_type=f32)


def prepare(blocks, t_left, t_right, s_left, s_right, s_feat):
    norms = []
    largest = jnp.zeros((1, ROWS), f32)
    for p in range(DP):
        x = blocks[p, 0:SW, :].astype(f32)
        square = jnp.sum(x * x, axis=0, keepdims=True)
        norms.append(square)
        largest = jnp.maximum(largest, square)
    largest = jnp.max(largest, axis=1, keepdims=True)
    first = lax.broadcasted_iota(jnp.int32, (16, ROWS), 0) == 0
    ones = jnp.where(first, 1.0, 0.0)
    zeros = jnp.zeros((16, ROWS), f32)
    for p in range(DP):
        rows = slice(p * ROWS, (p + 1) * ROWS)
        features = blocks[p, 0:SW, :]
        x = features.astype(f32)
        scaled = x * S_SCALE
        high = scaled.astype(bf16)
        low = (scaled - high.astype(f32)).astype(bf16)
        shift = (0.5 * S_SCALE) * (jnp.sqrt(norms[p] * largest) + norms[p])
        shift = jnp.where(first, -shift, 0.0).astype(bf16)
        s_right[:, rows] = jnp.concatenate([high, low, shift, zeros.astype(bf16)], axis=0)
        s_left[rows, :] = jnp.concatenate([x, x, ones, zeros], axis=0).T.astype(bf16)
        s_feat[:, rows] = features
        x = blocks[p, SW:, :]
        scaled = x.astype(f32) * T_SCALE
        high = scaled.astype(bf16)
        t_left[rows, 0:TW] = x
        t_left[rows, TW:] = x
        t_right[rows, 0:TW] = high
        t_right[rows, TW:] = (scaled - high.astype(f32)).astype(bf16)


def fold(x, op):
    parts = [x[8 * n : 8 * n + 8, :] for n in range(x.shape[0] // 8)]
    while len(parts) > 1:
        parts = [op(*parts[n : n + 2]) if n + 1 < len(parts) else parts[n] for n in range(0, len(parts), 2)]
    return parts[0]


def pipeline_step(scores, exps, grads, work):
    t_raw, s_raw, t_exp, s_exp, t_top, gain, kl = work
    repeat = PIECE // 8
    if grads is not None:
        (s_feat, total), block = grads
        last = pl.ds(pl.multiple_of(block * BLOCK, BLOCK), BLOCK)
        x_last = s_feat[:, last]
        s_gain = jnp.concatenate([gain[COUNT * 8 :, :]] * repeat, axis=0)
        t_gain = [gain[k * 8 : k * 8 + 8, :] for k in range(COUNT)]
        forward = jnp.zeros((SW, BLOCK), f32)
    if exps:
        t_max = [t_top[k * 8 : k * 8 + 8, :] for k in range(COUNT)]
        t_sum, cross = [], []
        s_sum = jnp.zeros((8, BLOCK), f32)
    if scores is not None:
        (t_left, t_right, s_left, s_right), block = scores
        own = pl.ds(pl.multiple_of(block * BLOCK, BLOCK), BLOCK)
        t_own = t_right[own, :]
        s_own = s_right[:, own]
    for k in range(COUNT):
        part = slice(k * CHUNK, (k + 1) * CHUNK)
        pieces = [slice(n, n + PIECE) for n in range(k * CHUNK, (k + 1) * CHUNK, PIECE)]
        if grads is not None:
            t_wide = jnp.concatenate([t_gain[k]] * repeat, axis=0)
            grad = jnp.concatenate(
                [(s_exp[n, :] * s_gain - t_exp[n, :] * t_wide).astype(bf16) for n in pieces], axis=0
            )
            forward = forward + dot_nn(s_feat[:, part], grad)
            total[:, part] += dot_nt(x_last, grad)
        if exps:
            top_wide = jnp.concatenate([t_max[k]] * repeat, axis=0)
            z = jnp.zeros((8, BLOCK), f32)
            c = jnp.zeros((8, BLOCK), f32)
            for n in pieces:
                t = t_raw[n, :] - top_wide
                s = s_raw[n, :]
                te = jnp.exp2(t)
                se = jnp.exp2(s)
                z = z + fold(te, jnp.add)
                s_sum = s_sum + fold(se, jnp.add)
                c = c + fold(te * (t - s), jnp.add)
                t_exp[n, :] = te
                s_exp[n, :] = se
            t_sum.append(z)
            cross.append(c)
        if scores is not None:
            t_all = dot_nt(t_left[part, :], t_own)
            t_raw[part, :] = t_all
            t_top[k * 8 : k * 8 + 8, :] = fold(t_all, jnp.maximum)
            s_raw[part, :] = dot_nn(s_left[part, :], s_own)
    if grads is not None:
        total[:, last] += forward
    if exps:
        top = functools.reduce(jnp.maximum, t_max)
        top = jnp.broadcast_to(jnp.max(top, axis=0, keepdims=True), (8, BLOCK))
        lift = [jnp.exp2(x - top) for x in t_max]
        z = sum(f * x for f, x in zip(lift, t_sum))
        c = sum(f * (c + (m - top) * x) for f, c, m, x in zip(lift, cross, t_max, t_sum))
        z = jnp.sum(z, axis=0, keepdims=True)
        c = jnp.sum(c, axis=0, keepdims=True)
        s_sum = jnp.sum(s_sum, axis=0, keepdims=True)
        kl[...] += math.log(2.0) * c / z - jnp.log(z) + jnp.log(s_sum)
        t_gain = jnp.broadcast_to(LOSS_SCALE / z, (8, BLOCK))
        for k in range(COUNT):
            gain[k * 8 : k * 8 + 8, :] = t_gain * lift[k]
        gain[COUNT * 8 :, :] = jnp.broadcast_to(LOSS_SCALE / s_sum, (8, BLOCK))


def kernel(
    teacher_hbm, student_hbm, loss_out, grads_out,
    t_in, s_in, send, got, g_send, g_got,
    t_left, t_right, s_left, s_right, s_feat, total,
    t_raw, s_raw, t_exp, s_exp, t_top, gain, kl,
    loss_a, loss_b,
    load_sem, send_sem, got_sem, g_send_sem, g_got_sem, loss_send_sem, loss_got_sem,
):
    me = lax.axis_index("dp")
    lane = lax.axis_index("tensor")

    def loads(r):
        return (
            pltpu.make_async_copy(student_hbm.at[r], s_in.at[r], load_sem.at[1, r]),
            pltpu.make_async_copy(teacher_hbm.at[r], t_in.at[r], load_sem.at[0, r]),
        )

    for r in range(RELATIONS):
        for copy in loads(r):
            copy.start()

    barrier = pltpu.get_barrier_semaphore()

    def greet_dp(n, carry):
        pl.semaphore_signal(barrier, inc=1, device_id={"dp": lax.rem(me + n, DP)}, device_id_type=MESH)
        return carry

    def greet_tensor(n, carry):
        pl.semaphore_signal(barrier, inc=1, device_id={"tensor": lax.rem(lane + n, TENSOR)}, device_id_type=MESH)
        return carry

    lax.fori_loop(1, DP, greet_dp, 0)
    lax.fori_loop(1, TENSOR, greet_tensor, 0)

    def pack(r):
        student, teacher = loads(r)
        student.wait()
        for s in range(SEQS):
            x = s_in[r, :, s, :].astype(f32).T.astype(bf16)
            for a in range(HEADS):
                send[r, s * HEADS + a, 0:SW, :] = x[a * SW : (a + 1) * SW, :]
        teacher.wait()
        for s in range(SEQS):
            x = t_in[r, :, s, :]
            for a in range(HEADS):
                send[r, s * HEADS + a, SW:, :] = x[:, a * TW : (a + 1) * TW]

    def send_blocks(source, target, source_sem, target_sem, r):
        def one(n, carry):
            to = lax.rem(me + n, DP)
            pltpu.make_async_remote_copy(
                src_ref=source.at[r, to],
                dst_ref=target.at[r, me],
                send_sem=source_sem.at[r],
                recv_sem=target_sem.at[r],
                device_id={"dp": to},
                device_id_type=MESH,
            ).start()
            return carry

        lax.fori_loop(1, DP, one, 0)
        target[r, me] = source[r, me]

    def wait_blocks(buffer, sem, r):
        span = buffer.at[r, pl.ds(0, DP - 1)]
        pltpu.make_async_copy(span, span, sem.at[r]).wait()

    def place(r):
        wait_blocks(g_got, g_got_sem, r)
        for s in range(SEQS):
            x = g_got[r, s * HEADS : (s + 1) * HEADS].reshape(HEADS * SW, ROWS)
            grads_out[r, :, s, :] = x.T

    def receive(r):
        wait_blocks(got, got_sem, r)
        half = lax.rem(r, 2)
        prepare(got.at[r], t_left.at[half], t_right.at[half], s_left.at[half], s_right.at[half], s_feat.at[half])

    def round_grads(r):
        half = lax.rem(r, 2)
        for p in range(DP):
            g_send[r, p] = (total[half, :, p * ROWS : (p + 1) * ROWS] * (1.0 / math.sqrt(SW))).astype(bf16)

    def give_back(r):
        send_blocks(g_send, g_got, g_send_sem, g_got_sem, r)

    def for_scores(n):
        half = lax.rem(n // BLOCKS, 2)
        return (t_left.at[half], t_right.at[half], s_left.at[half], s_right.at[half]), lax.rem(n, BLOCKS)

    def for_grads(n):
        half = lax.rem(n // BLOCKS, 2)
        return (s_feat.at[half], total.at[half]), lax.rem(n, BLOCKS)

    work = (t_raw, s_raw, t_exp, s_exp, t_top, gain, kl)

    pack(0)
    pl.semaphore_wait(barrier, DP - 1 + TENSOR - 1)
    send_blocks(send, got, send_sem, got_sem, 0)
    pack(1)
    pack(2)
    kl[...] = jnp.zeros_like(kl)
    gain[...] = jnp.zeros_like(gain)
    t_exp[...] = jnp.zeros_like(t_exp)
    s_exp[...] = jnp.zeros_like(s_exp)
    s_feat[1] = jnp.zeros_like(s_feat[1])
    total[...] = jnp.zeros_like(total)
    send_blocks(send, got, send_sem, got_sem, 1)
    receive(0)
    pipeline_step(for_scores(0), False, None, work)

    def step(n, carry):
        block = lax.rem(n, BLOCKS)
        r = n // BLOCKS

        @pl.when(n == 0)
        def _():
            send_blocks(send, got, send_sem, got_sem, 2)

        @pl.when((block == BLOCKS - 1) & (r < RELATIONS - 1))
        def _():
            receive(r + 1)

        pipeline_step(for_scores(n + 1), True, for_grads(n + 2 * BLOCKS - 1), work)

        @pl.when((block == 0) & (r > 0))
        def _():
            round_grads(r - 1)
            give_back(r - 1)

        @pl.when((block == 0) & (r < RELATIONS - 1))
        def _():
            half = lax.rem(r + 1, 2)
            total[half] = jnp.zeros((SW, LENGTH), f32)

        return carry

    lax.fori_loop(0, RELATIONS * BLOCKS - 1, step, 0)
    pipeline_step(None, True, for_grads(RELATIONS * BLOCKS - 2), work)

    def share(buffer, axis, here, size, which, value):
        buffer[here] = value

        def one(n, carry):
            to = lax.rem(here + n, size)
            pltpu.make_async_remote_copy(
                src_ref=buffer.at[here],
                dst_ref=buffer.at[here],
                send_sem=loss_send_sem.at[which],
                recv_sem=loss_got_sem.at[which],
                device_id={axis: to},
                device_id_type=MESH,
            ).start()
            return carry

        lax.fori_loop(1, size, one, 0)

    def collect(buffer, size, which):
        span = buffer.at[pl.ds(0, size - 1)]
        pltpu.make_async_copy(span, span, loss_got_sem.at[which]).wait()
        return functools.reduce(lambda a, b: a + b, [buffer[n] for n in range(size)])

    part = jnp.broadcast_to(jnp.sum(kl[...], axis=1, keepdims=True), (8, 128))
    share(loss_a, "dp", me, DP, 0, part)
    pipeline_step(None, False, for_grads(RELATIONS * BLOCKS - 1), work)
    round_grads(RELATIONS - 1)
    share(loss_b, "tensor", lane, TENSOR, 1, collect(loss_a, DP, 0))
    give_back(RELATIONS - 1)
    for r in range(RELATIONS - 1):
        place(r)
    loss_out[...] = collect(loss_b, TENSOR, 1) * (1.0 / (RELATIONS * SEQS * RH * LENGTH))
    for r in range(RELATIONS):
        wait_blocks(send, send_sem, r)
        wait_blocks(g_send, g_send_sem, r)
    for which, buffer, size in ((0, loss_a, DP), (1, loss_b, TENSOR)):
        span = buffer.at[pl.ds(0, size - 1)]
        pltpu.make_async_copy(span, span, loss_send_sem.at[which]).wait()
    place(RELATIONS - 1)


def per_device(teacher_states, student_states):
    dma = pltpu.SemaphoreType.DMA
    loss, grads = pl.pallas_call(
        kernel,
        out_shape=(
            jax.ShapeDtypeStruct((8, 128), f32),
            jax.ShapeDtypeStruct(student_states.shape, bf16),
        ),
        in_specs=[pl.BlockSpec(memory_space=pl.ANY)] * 2,
        out_specs=(pl.BlockSpec(memory_space=pltpu.VMEM), pl.BlockSpec(memory_space=pltpu.VMEM)),
        scratch_shapes=[
            pltpu.VMEM((RELATIONS, ROWS, SEQS, HEADS * TW), bf16),
            pltpu.VMEM((RELATIONS, ROWS, SEQS, HEADS * SW), bf16),
            pltpu.VMEM((RELATIONS, DP, SW + ROWS, 128), bf16),
            pltpu.VMEM((RELATIONS, DP, SW + ROWS, 128), bf16),
            pltpu.VMEM((RELATIONS, DP, SW, ROWS), bf16),
            pltpu.VMEM((RELATIONS, DP, SW, ROWS), bf16),
            pltpu.VMEM((2, LENGTH, 2 * TW), bf16),
            pltpu.VMEM((2, LENGTH, 2 * TW), bf16),
            pltpu.VMEM((2, LENGTH, 128), bf16),
            pltpu.VMEM((2, 128, LENGTH), bf16),
            pltpu.VMEM((2, SW, LENGTH), bf16),
            pltpu.VMEM((2, SW, LENGTH), f32),
            pltpu.VMEM((LENGTH, BLOCK), f32),
            pltpu.VMEM((LENGTH, BLOCK), f32),
            pltpu.VMEM((LENGTH, BLOCK), f32),
            pltpu.VMEM((LENGTH, BLOCK), f32),
            pltpu.VMEM((8 * COUNT, BLOCK), f32),
            pltpu.VMEM((8 * (COUNT + 1), BLOCK), f32),
            pltpu.VMEM((1, BLOCK), f32),
            pltpu.VMEM((DP, 8, 128), f32),
            pltpu.VMEM((TENSOR, 8, 128), f32),
            dma((2, RELATIONS)),
            dma((RELATIONS,)),
            dma((RELATIONS,)),
            dma((RELATIONS,)),
            dma((RELATIONS,)),
            dma((2,)),
            dma((2,)),
        ],
        compiler_params=pltpu.CompilerParams(
            collective_id=0, has_side_effects=True, vmem_limit_bytes=54400 * 1024
        ),
    )(teacher_states, student_states)
    return loss[0, 0], grads


def solution(mesh):
    placed = (P(None, "dp", None, "tensor"), P(None, "dp", None, "tensor"))
    return jax.shard_map(
        per_device,
        mesh=mesh,
        in_specs=placed,
        out_specs=(P(), P(None, "dp", None, "tensor")),
        check_vma=False,
    )
```

```python
import functools
import math

import jax
import jax.numpy as jnp
from jax import lax
from jax.experimental import pallas as pl
from jax.experimental.pallas import tpu as pltpu
from jax.sharding import PartitionSpec as P

RELATIONS = 3
SEQS = 2
RH = 64
LENGTH = 2048
TW = 128
SW = 48
DP = 16
TENSOR = 8
ROWS = LENGTH // DP
HEADS = RH // TENSOR
BLOCK = 256
BLOCKS = LENGTH // BLOCK
CHUNK = 512
COUNT = LENGTH // CHUNK
PIECE = 32
LOSS_SCALE = 16.0
LOG2E = 1.0 / math.log(2.0)
T_SCALE = LOG2E / math.sqrt(TW)
S_SCALE = LOG2E / math.sqrt(SW)
MESH = pl.DeviceIdType.MESH
f32 = jnp.float32
bf16 = jnp.bfloat16


def dot_nt(a, b):
    return lax.dot_general(a, b, (((1,), (1,)), ((), ())), preferred_element_type=f32)


def dot_nn(a, b):
    return jnp.dot(a, b, preferred_element_type=f32)


def prepare(blocks, t_left, t_right, s_left, s_right, s_feat):
    norms = []
    largest = jnp.zeros((1, ROWS), f32)
    for p in range(DP):
        x = blocks[p, 0:SW, :].astype(f32)
        square = jnp.sum(x * x, axis=0, keepdims=True)
        norms.append(square)
        largest = jnp.maximum(largest, square)
    largest = jnp.max(largest, axis=1, keepdims=True)
    first = lax.broadcasted_iota(jnp.int32, (16, ROWS), 0) == 0
    ones = jnp.where(first, 1.0, 0.0)
    zeros = jnp.zeros((16, ROWS), f32)
    for p in range(DP):
        rows = slice(p * ROWS, (p + 1) * ROWS)
        features = blocks[p, 0:SW, :]
        x = features.astype(f32)
        scaled = x * S_SCALE
        high = scaled.astype(bf16)
        low = (scaled - high.astype(f32)).astype(bf16)
        shift = (0.5 * S_SCALE) * (jnp.sqrt(norms[p] * largest) + norms[p])
        shift = jnp.where(first, -shift, 0.0).astype(bf16)
        s_right[:, rows] = jnp.concatenate([high, low, shift, zeros.astype(bf16)], axis=0)
        s_left[rows, :] = jnp.concatenate([x, x, ones, zeros], axis=0).T.astype(bf16)
        s_feat[:, rows] = features
        x = blocks[p, SW:, :]
        scaled = x.astype(f32) * T_SCALE
        high = scaled.astype(bf16)
        t_left[rows, 0:TW] = x
        t_left[rows, TW:] = x
        t_right[rows, 0:TW] = high
        t_right[rows, TW:] = (scaled - high.astype(f32)).astype(bf16)


def fold(x, op):
    parts = [x[8 * n : 8 * n + 8, :] for n in range(x.shape[0] // 8)]
    while len(parts) > 1:
        parts = [op(*parts[n : n + 2]) if n + 1 < len(parts) else parts[n] for n in range(0, len(parts), 2)]
    return parts[0]


def pipeline_step(scores, exps, grads, work):
    t_raw, s_raw, t_exp, s_exp, t_top, gain, kl = work
    repeat = PIECE // 8
    if grads is not None:
        (s_feat, total), block = grads
        last = pl.ds(pl.multiple_of(block * BLOCK, BLOCK), BLOCK)
        x_last = s_feat[:, last]
        s_gain = jnp.concatenate([gain[COUNT * 8 :, :]] * repeat, axis=0)
        t_gain = [gain[k * 8 : k * 8 + 8, :] for k in range(COUNT)]
        forward = jnp.zeros((SW, BLOCK), f32)
    if exps:
        t_max = [t_top[k * 8 : k * 8 + 8, :] for k in range(COUNT)]
        t_sum, cross = [], []
        s_sum = jnp.zeros((8, BLOCK), f32)
    if scores is not None:
        (t_left, t_right, s_left, s_right), block = scores
        own = pl.ds(pl.multiple_of(block * BLOCK, BLOCK), BLOCK)
        t_own = t_right[own, :]
        s_own = s_right[:, own]
    for k in range(COUNT):
        part = slice(k * CHUNK, (k + 1) * CHUNK)
        pieces = [slice(n, n + PIECE) for n in range(k * CHUNK, (k + 1) * CHUNK, PIECE)]
        if grads is not None:
            t_wide = jnp.concatenate([t_gain[k]] * repeat, axis=0)
            grad = jnp.concatenate(
                [(s_exp[n, :] * s_gain - t_exp[n, :] * t_wide).astype(bf16) for n in pieces], axis=0
            )
            forward = forward + dot_nn(s_feat[:, part], grad)
            total[:, part] += dot_nt(x_last, grad)
        if exps:
            top_wide = jnp.concatenate([t_max[k]] * repeat, axis=0)
            z = jnp.zeros((8, BLOCK), f32)
            c = jnp.zeros((8, BLOCK), f32)
            for n in pieces:
                t = t_raw[n, :] - top_wide
                s = s_raw[n, :]
                te = jnp.exp2(t)
                se = jnp.exp2(s)
                z = z + fold(te, jnp.add)
                s_sum = s_sum + fold(se, jnp.add)
                c = c + fold(te * (t - s), jnp.add)
                t_exp[n, :] = te
                s_exp[n, :] = se
            t_sum.append(z)
            cross.append(c)
        if scores is not None:
            t_all = dot_nt(t_left[part, :], t_own)
            t_raw[part, :] = t_all
            t_top[k * 8 : k * 8 + 8, :] = fold(t_all, jnp.maximum)
            s_raw[part, :] = dot_nn(s_left[part, :], s_own)
    if grads is not None:
        total[:, last] += forward
    if exps:
        top = functools.reduce(jnp.maximum, t_max)
        top = jnp.broadcast_to(jnp.max(top, axis=0, keepdims=True), (8, BLOCK))
        lift = [jnp.exp2(x - top) for x in t_max]
        z = sum(f * x for f, x in zip(lift, t_sum))
        c = sum(f * (c + (m - top) * x) for f, c, m, x in zip(lift, cross, t_max, t_sum))
        z = jnp.sum(z, axis=0, keepdims=True)
        c = jnp.sum(c, axis=0, keepdims=True)
        s_sum = jnp.sum(s_sum, axis=0, keepdims=True)
        kl[...] += math.log(2.0) * c / z - jnp.log(z) + jnp.log(s_sum)
        t_gain = jnp.broadcast_to(LOSS_SCALE / z, (8, BLOCK))
        for k in range(COUNT):
            gain[k * 8 : k * 8 + 8, :] = t_gain * lift[k]
        gain[COUNT * 8 :, :] = jnp.broadcast_to(LOSS_SCALE / s_sum, (8, BLOCK))


def kernel(
    teacher_hbm, student_hbm, loss_out, grads_out,
    t_in, s_in, send, got, g_send, g_got,
    t_left, t_right, s_left, s_right, s_feat, total,
    t_raw, s_raw, t_exp, s_exp, t_top, gain, kl,
    loss_a, loss_b,
    load_sem, send_sem, got_sem, g_send_sem, g_got_sem, loss_send_sem, loss_got_sem,
):
    me = lax.axis_index("dp")
    lane = lax.axis_index("tensor")

    def loads(r):
        return (
            pltpu.make_async_copy(student_hbm.at[r], s_in.at[r], load_sem.at[1, r]),
            pltpu.make_async_copy(teacher_hbm.at[r], t_in.at[r], load_sem.at[0, r]),
        )

    for r in range(RELATIONS):
        for copy in loads(r):
            copy.start()

    barrier = pltpu.get_barrier_semaphore()

    def greet_dp(n, carry):
        pl.semaphore_signal(barrier, inc=1, device_id={"dp": lax.rem(me + n, DP)}, device_id_type=MESH)
        return carry

    def greet_tensor(n, carry):
        pl.semaphore_signal(barrier, inc=1, device_id={"tensor": lax.rem(lane + n, TENSOR)}, device_id_type=MESH)
        return carry

    lax.fori_loop(1, DP, greet_dp, 0)
    lax.fori_loop(1, TENSOR, greet_tensor, 0)

    def pack(r, s):
        x = s_in[r, :, s, :].astype(f32).T.astype(bf16)
        for a in range(HEADS):
            send[r, SEQS * a + s, 0:SW, :] = x[a * SW : (a + 1) * SW, :]
        x = t_in[r, :, s, :]
        for a in range(HEADS):
            send[r, SEQS * a + s, SW:, :] = x[:, a * TW : (a + 1) * TW]

    def send_one(source, target, source_sem, target_sem, r, to):
        pltpu.make_async_remote_copy(
            src_ref=source.at[r, to],
            dst_ref=target.at[r, me],
            send_sem=source_sem.at[r],
            recv_sem=target_sem.at[r],
            device_id={"dp": to},
            device_id_type=MESH,
        ).start()

    def send_blocks(source, target, source_sem, target_sem, r, low=1, high=DP):
        def one(n, carry):
            send_one(source, target, source_sem, target_sem, r, lax.rem(me + n, DP))
            return carry

        lax.fori_loop(low, high, one, 0)

    def send_half(r, s):
        odd = lax.rem(me + s, SEQS)

        def one(n, carry):
            send_one(send, got, send_sem, got_sem, r, lax.rem(me + odd + SEQS * n, DP))
            return carry

        lax.fori_loop(1 - odd, HEADS, one, 0)

    def wait_blocks(buffer, sem, r):
        span = buffer.at[r, pl.ds(0, DP - 1)]
        pltpu.make_async_copy(span, span, sem.at[r]).wait()

    def place(r):
        g_got[r, me] = g_send[r, me]
        wait_blocks(g_got, g_got_sem, r)
        for s in range(SEQS):
            x = jnp.concatenate([g_got[r, SEQS * a + s] for a in range(HEADS)], axis=0)
            grads_out[r, :, s, :] = x.T

    def receive(r):
        got[r, me] = send[r, me]
        wait_blocks(got, got_sem, r)
        half = lax.rem(r, 2)
        prepare(got.at[r], t_left.at[half], t_right.at[half], s_left.at[half], s_right.at[half], s_feat.at[half])

    def round_grads(r):
        half = lax.rem(r, 2)
        for p in range(DP):
            g_send[r, p] = (total[half, :, p * ROWS : (p + 1) * ROWS] * (1.0 / math.sqrt(SW))).astype(bf16)

    def give_back(r, low=1, high=DP):
        send_blocks(g_send, g_got, g_send_sem, g_got_sem, r, low, high)

    def for_scores(n):
        half = lax.rem(n // BLOCKS, 2)
        return (t_left.at[half], t_right.at[half], s_left.at[half], s_right.at[half]), lax.rem(n, BLOCKS)

    def for_grads(n):
        half = lax.rem(n // BLOCKS, 2)
        return (s_feat.at[half], total.at[half]), lax.rem(n, BLOCKS)

    work = (t_raw, s_raw, t_exp, s_exp, t_top, gain, kl)

    for copy in loads(0):
        copy.wait()
    pack(0, 0)
    pl.semaphore_wait(barrier, DP - 1 + TENSOR - 1)
    send_half(0, 0)
    pack(0, 1)
    send_half(0, 1)
    for r in range(1, RELATIONS):
        for copy in loads(r):
            copy.wait()
        for s in range(SEQS):
            pack(r, s)
    kl[...] = jnp.zeros_like(kl)
    gain[...] = jnp.zeros_like(gain)
    t_exp[...] = jnp.zeros_like(t_exp)
    s_exp[...] = jnp.zeros_like(s_exp)
    s_feat[1] = jnp.zeros_like(s_feat[1])
    total[...] = jnp.zeros_like(total)
    send_blocks(send, got, send_sem, got_sem, 1)
    receive(0)
    pipeline_step(for_scores(0), False, None, work)

    def step(n, carry):
        block = lax.rem(n, BLOCKS)
        r = n // BLOCKS

        @pl.when(n == 0)
        def _():
            send_blocks(send, got, send_sem, got_sem, 2)

        @pl.when((block == BLOCKS - 1) & (r < RELATIONS - 1))
        def _():
            receive(r + 1)

        pipeline_step(for_scores(n + 1), True, for_grads(n + 2 * BLOCKS - 1), work)

        @pl.when((block == 0) & (r > 0))
        def _():
            round_grads(r - 1)
            give_back(r - 1)

        @pl.when((block == 0) & (r < RELATIONS - 1))
        def _():
            half = lax.rem(r + 1, 2)
            total[half] = jnp.zeros((SW, LENGTH), f32)

        return carry

    lax.fori_loop(0, RELATIONS * BLOCKS - 1, step, 0)
    pipeline_step(None, True, for_grads(RELATIONS * BLOCKS - 2), work)

    def share(buffer, axis, here, size, which, value):
        buffer[here] = value

        def one(n, carry):
            to = lax.rem(here + n, size)
            pltpu.make_async_remote_copy(
                src_ref=buffer.at[here],
                dst_ref=buffer.at[here],
                send_sem=loss_send_sem.at[which],
                recv_sem=loss_got_sem.at[which],
                device_id={axis: to},
                device_id_type=MESH,
            ).start()
            return carry

        lax.fori_loop(1, size, one, 0)

    def collect(buffer, size, which):
        span = buffer.at[pl.ds(0, size - 1)]
        pltpu.make_async_copy(span, span, loss_got_sem.at[which]).wait()
        return functools.reduce(lambda a, b: a + b, [buffer[n] for n in range(size)])

    part = jnp.broadcast_to(jnp.sum(kl[...], axis=1, keepdims=True), (8, 128))
    share(loss_a, "dp", me, DP, 0, part)
    pipeline_step(None, False, for_grads(RELATIONS * BLOCKS - 1), work)
    round_grads(RELATIONS - 1)
    give_back(RELATIONS - 1, 1, DP // 2)
    share(loss_b, "tensor", lane, TENSOR, 1, collect(loss_a, DP, 0))
    give_back(RELATIONS - 1, DP // 2, DP)
    for r in range(RELATIONS - 1):
        place(r)
    loss_out[...] = collect(loss_b, TENSOR, 1) * (1.0 / (RELATIONS * SEQS * RH * LENGTH))
    for r in range(RELATIONS):
        wait_blocks(send, send_sem, r)
        wait_blocks(g_send, g_send_sem, r)
    for which, buffer, size in ((0, loss_a, DP), (1, loss_b, TENSOR)):
        span = buffer.at[pl.ds(0, size - 1)]
        pltpu.make_async_copy(span, span, loss_send_sem.at[which]).wait()
    place(RELATIONS - 1)


def per_device(teacher_states, student_states):
    dma = pltpu.SemaphoreType.DMA
    loss, grads = pl.pallas_call(
        kernel,
        out_shape=(
            jax.ShapeDtypeStruct((8, 128), f32),
            jax.ShapeDtypeStruct(student_states.shape, bf16),
        ),
        in_specs=[pl.BlockSpec(memory_space=pl.ANY)] * 2,
        out_specs=(pl.BlockSpec(memory_space=pltpu.VMEM), pl.BlockSpec(memory_space=pltpu.VMEM)),
        scratch_shapes=[
            pltpu.VMEM((RELATIONS, ROWS, SEQS, HEADS * TW), bf16),
            pltpu.VMEM((RELATIONS, ROWS, SEQS, HEADS * SW), bf16),
            pltpu.VMEM((RELATIONS, DP, SW + ROWS, 128), bf16),
            pltpu.VMEM((RELATIONS, DP, SW + ROWS, 128), bf16),
            pltpu.VMEM((RELATIONS, DP, SW, ROWS), bf16),
            pltpu.VMEM((RELATIONS, DP, SW, ROWS), bf16),
            pltpu.VMEM((2, LENGTH, 2 * TW), bf16),
            pltpu.VMEM((2, LENGTH, 2 * TW), bf16),
            pltpu.VMEM((2, LENGTH, 128), bf16),
            pltpu.VMEM((2, 128, LENGTH), bf16),
            pltpu.VMEM((2, SW, LENGTH), bf16),
            pltpu.VMEM((2, SW, LENGTH), f32),
            pltpu.VMEM((LENGTH, BLOCK), f32),
            pltpu.VMEM((LENGTH, BLOCK), f32),
            pltpu.VMEM((LENGTH, BLOCK), f32),
            pltpu.VMEM((LENGTH, BLOCK), f32),
            pltpu.VMEM((8 * COUNT, BLOCK), f32),
            pltpu.VMEM((8 * (COUNT + 1), BLOCK), f32),
            pltpu.VMEM((1, BLOCK), f32),
            pltpu.VMEM((DP, 8, 128), f32),
            pltpu.VMEM((TENSOR, 8, 128), f32),
            dma((2, RELATIONS)),
            dma((RELATIONS,)),
            dma((RELATIONS,)),
            dma((RELATIONS,)),
            dma((RELATIONS,)),
            dma((2,)),
            dma((2,)),
        ],
        compiler_params=pltpu.CompilerParams(
            collective_id=0, has_side_effects=True, vmem_limit_bytes=54400 * 1024
        ),
    )(teacher_states, student_states)
    return loss[0, 0], grads


def solution(mesh):
    placed = (P(None, "dp", None, "tensor"), P(None, "dp", None, "tensor"))
    return jax.shard_map(
        per_device,
        mesh=mesh,
        in_specs=placed,
        out_specs=(P(), P(None, "dp", None, "tensor")),
        check_vma=False,
    )
```

```python
import functools
import math

import jax
import jax.numpy as jnp
from jax import lax
from jax.experimental import pallas as pl
from jax.experimental.pallas import tpu as pltpu
from jax.sharding import PartitionSpec as P

RELATIONS = 3
SEQS = 2
RH = 64
LENGTH = 2048
TW = 128
SW = 48
DP = 16
TENSOR = 8
ROWS = LENGTH // DP
HEADS = RH // TENSOR
BLOCK = 256
BLOCKS = LENGTH // BLOCK
CHUNK = 512
COUNT = LENGTH // CHUNK
PIECE = 32
LOSS_SCALE = 16.0
LOG2E = 1.0 / math.log(2.0)
T_SCALE = LOG2E / math.sqrt(TW)
S_SCALE = LOG2E / math.sqrt(SW)
MESH = pl.DeviceIdType.MESH
f32 = jnp.float32
bf16 = jnp.bfloat16


def dot_nt(a, b):
    return lax.dot_general(a, b, (((1,), (1,)), ((), ())), preferred_element_type=f32)


def dot_nn(a, b):
    return jnp.dot(a, b, preferred_element_type=f32)


def prepare(blocks, t_left, t_right, s_left, s_right, s_feat):
    norms = []
    largest = jnp.zeros((1, ROWS), f32)
    for p in range(DP):
        x = blocks[p, 0:SW, :].astype(f32)
        square = jnp.sum(x * x, axis=0, keepdims=True)
        norms.append(square)
        largest = jnp.maximum(largest, square)
    largest = jnp.max(largest, axis=1, keepdims=True)
    first = lax.broadcasted_iota(jnp.int32, (16, ROWS), 0) == 0
    ones = jnp.where(first, 1.0, 0.0)
    zeros = jnp.zeros((16, ROWS), f32)
    for p in range(DP):
        rows = slice(p * ROWS, (p + 1) * ROWS)
        features = blocks[p, 0:SW, :]
        x = features.astype(f32)
        scaled = x * S_SCALE
        high = scaled.astype(bf16)
        low = (scaled - high.astype(f32)).astype(bf16)
        shift = (0.5 * S_SCALE) * (jnp.sqrt(norms[p] * largest) + norms[p])
        shift = jnp.where(first, -shift, 0.0).astype(bf16)
        s_right[:, rows] = jnp.concatenate([high, low, shift, zeros.astype(bf16)], axis=0)
        s_left[rows, :] = jnp.concatenate([x, x, ones, zeros], axis=0).T.astype(bf16)
        s_feat[:, rows] = features
        x = blocks[p, SW:, :]
        scaled = x.astype(f32) * T_SCALE
        high = scaled.astype(bf16)
        t_left[rows, 0:TW] = x
        t_left[rows, TW:] = x
        t_right[rows, 0:TW] = high
        t_right[rows, TW:] = (scaled - high.astype(f32)).astype(bf16)


def fold(x, op):
    parts = [x[8 * n : 8 * n + 8, :] for n in range(x.shape[0] // 8)]
    while len(parts) > 1:
        parts = [op(*parts[n : n + 2]) if n + 1 < len(parts) else parts[n] for n in range(0, len(parts), 2)]
    return parts[0]


def pipeline_step(scores, exps, grads, work):
    t_raw, s_raw, t_exp, s_exp, t_top, gain, kl = work
    repeat = PIECE // 8
    if grads is not None:
        (s_feat, total), block = grads
        last = pl.ds(pl.multiple_of(block * BLOCK, BLOCK), BLOCK)
        x_last = s_feat[:, last]
        s_gain = jnp.concatenate([gain[COUNT * 8 :, :]] * repeat, axis=0)
        t_gain = [gain[k * 8 : k * 8 + 8, :] for k in range(COUNT)]
        forward = jnp.zeros((SW, BLOCK), f32)
    if exps:
        t_max = [t_top[k * 8 : k * 8 + 8, :] for k in range(COUNT)]
        t_sum, cross = [], []
        s_sum = jnp.zeros((8, BLOCK), f32)
    if scores is not None:
        (t_left, t_right, s_left, s_right), block = scores
        own = pl.ds(pl.multiple_of(block * BLOCK, BLOCK), BLOCK)
        t_own = t_right[own, :]
        s_own = s_right[:, own]
    for k in range(COUNT):
        part = slice(k * CHUNK, (k + 1) * CHUNK)
        pieces = [slice(n, n + PIECE) for n in range(k * CHUNK, (k + 1) * CHUNK, PIECE)]
        if grads is not None:
            t_wide = jnp.concatenate([t_gain[k]] * repeat, axis=0)
            grad = jnp.concatenate(
                [(s_exp[n, :] * s_gain - t_exp[n, :] * t_wide).astype(bf16) for n in pieces], axis=0
            )
            forward = forward + dot_nn(s_feat[:, part], grad)
            total[:, part] += dot_nt(x_last, grad)
        if exps:
            top_wide = jnp.concatenate([t_max[k]] * repeat, axis=0)
            z = jnp.zeros((8, BLOCK), f32)
            c = jnp.zeros((8, BLOCK), f32)
            for n in pieces:
                t = t_raw[n, :] - top_wide
                s = s_raw[n, :]
                te = jnp.exp2(t)
                se = jnp.exp2(s)
                z = z + fold(te, jnp.add)
                s_sum = s_sum + fold(se, jnp.add)
                c = c + fold(te * (t - s), jnp.add)
                t_exp[n, :] = te
                s_exp[n, :] = se
            t_sum.append(z)
            cross.append(c)
        if scores is not None:
            t_all = dot_nt(t_left[part, :], t_own)
            t_raw[part, :] = t_all
            t_top[k * 8 : k * 8 + 8, :] = fold(t_all, jnp.maximum)
            s_raw[part, :] = dot_nn(s_left[part, :], s_own)
    if grads is not None:
        total[:, last] += forward
    if exps:
        top = functools.reduce(jnp.maximum, t_max)
        top = jnp.broadcast_to(jnp.max(top, axis=0, keepdims=True), (8, BLOCK))
        lift = [jnp.exp2(x - top) for x in t_max]
        z = sum(f * x for f, x in zip(lift, t_sum))
        c = sum(f * (c + (m - top) * x) for f, c, m, x in zip(lift, cross, t_max, t_sum))
        z = jnp.sum(z, axis=0, keepdims=True)
        c = jnp.sum(c, axis=0, keepdims=True)
        s_sum = jnp.sum(s_sum, axis=0, keepdims=True)
        kl[...] += math.log(2.0) * c / z - jnp.log(z) + jnp.log(s_sum)
        t_gain = jnp.broadcast_to(LOSS_SCALE / z, (8, BLOCK))
        for k in range(COUNT):
            gain[k * 8 : k * 8 + 8, :] = t_gain * lift[k]
        gain[COUNT * 8 :, :] = jnp.broadcast_to(LOSS_SCALE / s_sum, (8, BLOCK))


def kernel(
    teacher_hbm, student_hbm, loss_out, grads_out,
    t_in, s_in, send, got, g_send, g_got,
    t_left, t_right, s_left, s_right, s_feat, total,
    t_raw, s_raw, t_exp, s_exp, t_top, gain, kl,
    loss_a, loss_b,
    load_sem, send_sem, got_sem, g_send_sem, g_got_sem, loss_send_sem, loss_got_sem,
):
    me = lax.axis_index("dp")
    lane = lax.axis_index("tensor")

    def loads(r):
        return (
            pltpu.make_async_copy(student_hbm.at[r], s_in.at[r], load_sem.at[1, r]),
            pltpu.make_async_copy(teacher_hbm.at[r], t_in.at[r], load_sem.at[0, r]),
        )

    for r in range(RELATIONS):
        for copy in loads(r):
            copy.start()

    barrier = pltpu.get_barrier_semaphore()

    def greet_dp(n, carry):
        pl.semaphore_signal(barrier, inc=1, device_id={"dp": lax.rem(me + n, DP)}, device_id_type=MESH)
        return carry

    def greet_tensor(n, carry):
        pl.semaphore_signal(barrier, inc=1, device_id={"tensor": lax.rem(lane + n, TENSOR)}, device_id_type=MESH)
        return carry

    lax.fori_loop(1, DP, greet_dp, 0)
    lax.fori_loop(1, TENSOR, greet_tensor, 0)

    def pack(r, s):
        x = s_in[r, :, s, :].astype(f32).T.astype(bf16)
        for a in range(HEADS):
            send[r, SEQS * a + s, 0:SW, :] = x[a * SW : (a + 1) * SW, :]
        x = t_in[r, :, s, :]
        for a in range(HEADS):
            send[r, SEQS * a + s, SW:, :] = x[:, a * TW : (a + 1) * TW]

    def send_one(source, target, source_sem, target_sem, r, to):
        pltpu.make_async_remote_copy(
            src_ref=source.at[r, to],
            dst_ref=target.at[r, me],
            send_sem=source_sem.at[r],
            recv_sem=target_sem.at[r],
            device_id={"dp": to},
            device_id_type=MESH,
        ).start()

    def send_blocks(source, target, source_sem, target_sem, r, low=1, high=DP):
        def one(n, carry):
            send_one(source, target, source_sem, target_sem, r, lax.rem(me + n, DP))
            return carry

        lax.fori_loop(low, high, one, 0)

    def send_half(r, s):
        odd = lax.rem(me + s, SEQS)

        def one(n, carry):
            send_one(send, got, send_sem, got_sem, r, lax.rem(me + odd + SEQS * n, DP))
            return carry

        lax.fori_loop(1 - odd, HEADS, one, 0)

    def wait_blocks(buffer, sem, r):
        span = buffer.at[r, pl.ds(0, DP - 1)]
        pltpu.make_async_copy(span, span, sem.at[r]).wait()

    def place(r):
        g_got[r, me] = g_send[r, me]
        wait_blocks(g_got, g_got_sem, r)
        for s in range(SEQS):
            x = jnp.concatenate([g_got[r, SEQS * a + s] for a in range(HEADS)], axis=0)
            grads_out[r, :, s, :] = x.T

    def receive(r):
        got[r, me] = send[r, me]
        wait_blocks(got, got_sem, r)
        half = lax.rem(r, 2)
        prepare(got.at[r], t_left.at[half], t_right.at[half], s_left.at[half], s_right.at[half], s_feat.at[half])

    def round_grads(r):
        half = lax.rem(r, 2)
        for p in range(DP):
            g_send[r, p] = (total[half, :, p * ROWS : (p + 1) * ROWS] * (1.0 / math.sqrt(SW))).astype(bf16)

    def give_back(r, low=1, high=DP):
        send_blocks(g_send, g_got, g_send_sem, g_got_sem, r, low, high)

    def for_scores(n):
        half = lax.rem(n // BLOCKS, 2)
        return (t_left.at[half], t_right.at[half], s_left.at[half], s_right.at[half]), lax.rem(n, BLOCKS)

    def for_grads(n):
        half = lax.rem(n // BLOCKS, 2)
        return (s_feat.at[half], total.at[half]), lax.rem(n, BLOCKS)

    work = (t_raw, s_raw, t_exp, s_exp, t_top, gain, kl)

    for copy in loads(0):
        copy.wait()
    pack(0, 0)
    pl.semaphore_wait(barrier, DP - 1 + TENSOR - 1)
    send_half(0, 0)
    pack(0, 1)
    send_half(0, 1)
    for r in range(1, RELATIONS):
        for copy in loads(r):
            copy.wait()
        for s in range(SEQS):
            pack(r, s)
    kl[...] = jnp.zeros_like(kl)
    gain[...] = jnp.zeros_like(gain)
    t_exp[...] = jnp.zeros_like(t_exp)
    s_exp[...] = jnp.zeros_like(s_exp)
    s_feat[1] = jnp.zeros_like(s_feat[1])
    total[...] = jnp.zeros_like(total)
    receive(0)
    pipeline_step(for_scores(0), False, None, work)

    def step(n, carry):
        block = lax.rem(n, BLOCKS)
        r = n // BLOCKS

        for r_next, at in ((1, 0), (2, 5)):

            @pl.when(n == at)
            def _():
                send_blocks(send, got, send_sem, got_sem, r_next)

        @pl.when((block == BLOCKS - 1) & (r < RELATIONS - 1))
        def _():
            receive(r + 1)

        pipeline_step(for_scores(n + 1), True, for_grads(n + 2 * BLOCKS - 1), work)

        @pl.when((block == 0) & (r > 0))
        def _():
            round_grads(r - 1)
            give_back(r - 1)

        @pl.when((block == 0) & (r < RELATIONS - 1))
        def _():
            half = lax.rem(r + 1, 2)
            total[half] = jnp.zeros((SW, LENGTH), f32)

        return carry

    lax.fori_loop(0, RELATIONS * BLOCKS - 1, step, 0)
    pipeline_step(None, True, for_grads(RELATIONS * BLOCKS - 2), work)

    def share(buffer, axis, here, size, which, value):
        buffer[here] = value

        def one(n, carry):
            to = lax.rem(here + n, size)
            pltpu.make_async_remote_copy(
                src_ref=buffer.at[here],
                dst_ref=buffer.at[here],
                send_sem=loss_send_sem.at[which],
                recv_sem=loss_got_sem.at[which],
                device_id={axis: to},
                device_id_type=MESH,
            ).start()
            return carry

        lax.fori_loop(1, size, one, 0)

    def collect(buffer, size, which):
        span = buffer.at[pl.ds(0, size - 1)]
        pltpu.make_async_copy(span, span, loss_got_sem.at[which]).wait()
        return functools.reduce(lambda a, b: a + b, [buffer[n] for n in range(size)])

    part = jnp.broadcast_to(jnp.sum(kl[...], axis=1, keepdims=True), (8, 128))
    share(loss_a, "dp", me, DP, 0, part)
    pipeline_step(None, False, for_grads(RELATIONS * BLOCKS - 1), work)
    round_grads(RELATIONS - 1)
    give_back(RELATIONS - 1, 1, DP // 2)
    share(loss_b, "tensor", lane, TENSOR, 1, collect(loss_a, DP, 0))
    give_back(RELATIONS - 1, DP // 2, DP)
    for r in range(RELATIONS - 1):
        place(r)
    loss_out[...] = collect(loss_b, TENSOR, 1) * (1.0 / (RELATIONS * SEQS * RH * LENGTH))
    for r in range(RELATIONS):
        wait_blocks(send, send_sem, r)
        wait_blocks(g_send, g_send_sem, r)
    for which, buffer, size in ((0, loss_a, DP), (1, loss_b, TENSOR)):
        span = buffer.at[pl.ds(0, size - 1)]
        pltpu.make_async_copy(span, span, loss_send_sem.at[which]).wait()
    place(RELATIONS - 1)


def per_device(teacher_states, student_states):
    dma = pltpu.SemaphoreType.DMA
    loss, grads = pl.pallas_call(
        kernel,
        out_shape=(
            jax.ShapeDtypeStruct((8, 128), f32),
            jax.ShapeDtypeStruct(student_states.shape, bf16),
        ),
        in_specs=[pl.BlockSpec(memory_space=pl.ANY)] * 2,
        out_specs=(pl.BlockSpec(memory_space=pltpu.VMEM), pl.BlockSpec(memory_space=pltpu.VMEM)),
        scratch_shapes=[
            pltpu.VMEM((RELATIONS, ROWS, SEQS, HEADS * TW), bf16),
            pltpu.VMEM((RELATIONS, ROWS, SEQS, HEADS * SW), bf16),
            pltpu.VMEM((RELATIONS, DP, SW + ROWS, 128), bf16),
            pltpu.VMEM((RELATIONS, DP, SW + ROWS, 128), bf16),
            pltpu.VMEM((RELATIONS, DP, SW, ROWS), bf16),
            pltpu.VMEM((RELATIONS, DP, SW, ROWS), bf16),
            pltpu.VMEM((2, LENGTH, 2 * TW), bf16),
            pltpu.VMEM((2, LENGTH, 2 * TW), bf16),
            pltpu.VMEM((2, LENGTH, 128), bf16),
            pltpu.VMEM((2, 128, LENGTH), bf16),
            pltpu.VMEM((2, SW, LENGTH), bf16),
            pltpu.VMEM((2, SW, LENGTH), f32),
            pltpu.VMEM((LENGTH, BLOCK), f32),
            pltpu.VMEM((LENGTH, BLOCK), f32),
            pltpu.VMEM((LENGTH, BLOCK), f32),
            pltpu.VMEM((LENGTH, BLOCK), f32),
            pltpu.VMEM((8 * COUNT, BLOCK), f32),
            pltpu.VMEM((8 * (COUNT + 1), BLOCK), f32),
            pltpu.VMEM((1, BLOCK), f32),
            pltpu.VMEM((DP, 8, 128), f32),
            pltpu.VMEM((TENSOR, 8, 128), f32),
            dma((2, RELATIONS)),
            dma((RELATIONS,)),
            dma((RELATIONS,)),
            dma((RELATIONS,)),
            dma((RELATIONS,)),
            dma((2,)),
            dma((2,)),
        ],
        compiler_params=pltpu.CompilerParams(
            collective_id=0, has_side_effects=True, vmem_limit_bytes=54400 * 1024
        ),
    )(teacher_states, student_states)
    return loss[0, 0], grads


def solution(mesh):
    placed = (P(None, "dp", None, "tensor"), P(None, "dp", None, "tensor"))
    return jax.shard_map(
        per_device,
        mesh=mesh,
        in_specs=placed,
        out_specs=(P(), P(None, "dp", None, "tensor")),
        check_vma=False,
    )
```

```python
import functools
import math

import jax
import jax.numpy as jnp
from jax import lax
from jax.experimental import pallas as pl
from jax.experimental.pallas import tpu as pltpu
from jax.sharding import PartitionSpec as P

RELATIONS = 3
SEQS = 2
RH = 64
LENGTH = 2048
TW = 128
SW = 48
DP = 16
TENSOR = 8
ROWS = LENGTH // DP
HEADS = RH // TENSOR
BLOCK = 256
BLOCKS = LENGTH // BLOCK
CHUNK = 512
COUNT = LENGTH // CHUNK
PIECE = 32
LOSS_SCALE = 16.0
LOG2E = 1.0 / math.log(2.0)
T_SCALE = LOG2E / math.sqrt(TW)
S_SCALE = LOG2E / math.sqrt(SW)
MESH = pl.DeviceIdType.MESH
f32 = jnp.float32
bf16 = jnp.bfloat16


def dot_nt(a, b):
    return lax.dot_general(a, b, (((1,), (1,)), ((), ())), preferred_element_type=f32)


def dot_nn(a, b):
    return jnp.dot(a, b, preferred_element_type=f32)


def prepare(blocks, t_left, t_right, s_left, s_right, s_feat):
    norms = []
    largest = jnp.zeros((1, ROWS), f32)
    for p in range(DP):
        x = blocks[p, 0:SW, :].astype(f32)
        square = jnp.sum(x * x, axis=0, keepdims=True)
        norms.append(square)
        largest = jnp.maximum(largest, square)
    largest = jnp.max(largest, axis=1, keepdims=True)
    first = lax.broadcasted_iota(jnp.int32, (16, ROWS), 0) == 0
    ones = jnp.where(first, 1.0, 0.0)
    zeros = jnp.zeros((16, ROWS), f32)
    for p in range(DP):
        rows = slice(p * ROWS, (p + 1) * ROWS)
        features = blocks[p, 0:SW, :]
        x = features.astype(f32)
        scaled = x * S_SCALE
        high = scaled.astype(bf16)
        low = (scaled - high.astype(f32)).astype(bf16)
        shift = (0.5 * S_SCALE) * (jnp.sqrt(norms[p] * largest) + norms[p])
        shift = jnp.where(first, -shift, 0.0).astype(bf16)
        s_right[:, rows] = jnp.concatenate([high, low, shift, zeros.astype(bf16)], axis=0)
        s_left[rows, :] = jnp.concatenate([x, x, ones, zeros], axis=0).T.astype(bf16)
        s_feat[:, rows] = features
        x = blocks[p, SW:, :]
        scaled = x.astype(f32) * T_SCALE
        high = scaled.astype(bf16)
        t_left[rows, 0:TW] = x
        t_left[rows, TW:] = x
        t_right[rows, 0:TW] = high
        t_right[rows, TW:] = (scaled - high.astype(f32)).astype(bf16)


def fold(x, op):
    parts = [x[8 * n : 8 * n + 8, :] for n in range(x.shape[0] // 8)]
    while len(parts) > 1:
        parts = [op(*parts[n : n + 2]) if n + 1 < len(parts) else parts[n] for n in range(0, len(parts), 2)]
    return parts[0]


def pipeline_step(scores, exps, grads, work):
    t_raw, s_raw, t_exp, s_exp, t_top, gain, kl = work
    repeat = PIECE // 8
    if grads is not None:
        (s_feat, total), block = grads
        last = pl.ds(pl.multiple_of(block * BLOCK, BLOCK), BLOCK)
        x_last = s_feat[:, last]
        s_gain = jnp.concatenate([gain[COUNT * 8 :, :]] * repeat, axis=0)
        t_gain = [gain[k * 8 : k * 8 + 8, :] for k in range(COUNT)]
        forward = jnp.zeros((SW, BLOCK), f32)
    if exps:
        t_max = [t_top[k * 8 : k * 8 + 8, :] for k in range(COUNT)]
        t_sum, cross = [], []
        s_sum = jnp.zeros((8, BLOCK), f32)
    if scores is not None:
        (t_left, t_right, s_left, s_right), block = scores
        own = pl.ds(pl.multiple_of(block * BLOCK, BLOCK), BLOCK)
        t_own = t_right[own, :]
        s_own = s_right[:, own]
    for k in range(COUNT):
        part = slice(k * CHUNK, (k + 1) * CHUNK)
        pieces = [slice(n, n + PIECE) for n in range(k * CHUNK, (k + 1) * CHUNK, PIECE)]
        if grads is not None:
            t_wide = jnp.concatenate([t_gain[k]] * repeat, axis=0)
            grad = jnp.concatenate(
                [(s_exp[n, :] * s_gain - t_exp[n, :] * t_wide).astype(bf16) for n in pieces], axis=0
            )
            forward = forward + dot_nn(s_feat[:, part], grad)
            total[:, part] += dot_nt(x_last, grad)
        if exps:
            top_wide = jnp.concatenate([t_max[k]] * repeat, axis=0)
            z = jnp.zeros((8, BLOCK), f32)
            c = jnp.zeros((8, BLOCK), f32)
            for n in pieces:
                t = t_raw[n, :] - top_wide
                s = s_raw[n, :]
                te = jnp.exp2(t)
                se = jnp.exp2(s)
                z = z + fold(te, jnp.add)
                s_sum = s_sum + fold(se, jnp.add)
                c = c + fold(te * (t - s), jnp.add)
                t_exp[n, :] = te
                s_exp[n, :] = se
            t_sum.append(z)
            cross.append(c)
        if scores is not None:
            t_all = dot_nt(t_left[part, :], t_own)
            t_raw[part, :] = t_all
            t_top[k * 8 : k * 8 + 8, :] = fold(t_all, jnp.maximum)
            s_raw[part, :] = dot_nn(s_left[part, :], s_own)
    if grads is not None:
        total[:, last] += forward
    if exps:
        top = functools.reduce(jnp.maximum, t_max)
        top = jnp.broadcast_to(jnp.max(top, axis=0, keepdims=True), (8, BLOCK))
        lift = [jnp.exp2(x - top) for x in t_max]
        z = sum(f * x for f, x in zip(lift, t_sum))
        c = sum(f * (c + (m - top) * x) for f, c, m, x in zip(lift, cross, t_max, t_sum))
        z = jnp.sum(z, axis=0, keepdims=True)
        c = jnp.sum(c, axis=0, keepdims=True)
        s_sum = jnp.sum(s_sum, axis=0, keepdims=True)
        kl[...] += math.log(2.0) * c / z - jnp.log(z) + jnp.log(s_sum)
        t_gain = jnp.broadcast_to(LOSS_SCALE / z, (8, BLOCK))
        for k in range(COUNT):
            gain[k * 8 : k * 8 + 8, :] = t_gain * lift[k]
        gain[COUNT * 8 :, :] = jnp.broadcast_to(LOSS_SCALE / s_sum, (8, BLOCK))


def kernel(
    teacher_hbm, student_hbm, loss_out, grads_out,
    t_in, s_in, send, got, g_send, g_got,
    t_left, t_right, s_left, s_right, s_feat, total,
    t_raw, s_raw, t_exp, s_exp, t_top, gain, kl,
    loss_a, loss_b,
    load_sem, send_sem, got_sem, g_send_sem, g_got_sem, loss_send_sem, loss_got_sem,
):
    me = lax.axis_index("dp")
    lane = lax.axis_index("tensor")

    def loads(r):
        return (
            pltpu.make_async_copy(student_hbm.at[r], s_in.at[r], load_sem.at[1, r]),
            pltpu.make_async_copy(teacher_hbm.at[r], t_in.at[r], load_sem.at[0, r]),
        )

    for r in range(RELATIONS):
        for copy in loads(r):
            copy.start()

    barrier = pltpu.get_barrier_semaphore()

    def greet_dp(n, carry):
        pl.semaphore_signal(barrier, inc=1, device_id={"dp": lax.rem(me + n, DP)}, device_id_type=MESH)
        return carry

    def greet_tensor(n, carry):
        pl.semaphore_signal(barrier, inc=1, device_id={"tensor": lax.rem(lane + n, TENSOR)}, device_id_type=MESH)
        return carry

    lax.fori_loop(1, DP, greet_dp, 0)
    lax.fori_loop(1, TENSOR, greet_tensor, 0)

    def pack(r, s):
        x = s_in[r, :, s, :].astype(f32).T.astype(bf16)
        for a in range(HEADS):
            send[r, SEQS * a + s, 0:SW, :] = x[a * SW : (a + 1) * SW, :]
        x = t_in[r, :, s, :]
        for a in range(HEADS):
            send[r, SEQS * a + s, SW:, :] = x[:, a * TW : (a + 1) * TW]

    def send_one(source, target, source_sem, target_sem, r, to):
        pltpu.make_async_remote_copy(
            src_ref=source.at[r, to],
            dst_ref=target.at[r, me],
            send_sem=source_sem.at[r],
            recv_sem=target_sem.at[r],
            device_id={"dp": to},
            device_id_type=MESH,
        ).start()

    def send_blocks(source, target, source_sem, target_sem, r, low=1, high=DP):
        def one(n, carry):
            send_one(source, target, source_sem, target_sem, r, lax.rem(me + n, DP))
            return carry

        lax.fori_loop(low, high, one, 0)

    def send_half(r, s):
        odd = lax.rem(me + s, SEQS)

        def one(n, carry):
            send_one(send, got, send_sem, got_sem, r, lax.rem(me + odd + SEQS * n, DP))
            return carry

        lax.fori_loop(1 - odd, HEADS, one, 0)

    def wait_blocks(buffer, sem, r):
        span = buffer.at[r, pl.ds(0, DP - 1)]
        pltpu.make_async_copy(span, span, sem.at[r]).wait()

    def place(r):
        g_got[r, me] = g_send[r, me]
        wait_blocks(g_got, g_got_sem, r)
        for s in range(SEQS):
            x = jnp.concatenate([g_got[r, SEQS * a + s] for a in range(HEADS)], axis=0)
            grads_out[r, :, s, :] = x.T

    def receive(r):
        got[r, me] = send[r, me]
        wait_blocks(got, got_sem, r)
        half = lax.rem(r, 2)
        prepare(got.at[r], t_left.at[half], t_right.at[half], s_left.at[half], s_right.at[half], s_feat.at[half])

    def round_grads(r):
        half = lax.rem(r, 2)
        for p in range(DP):
            g_send[r, p] = (total[half, :, p * ROWS : (p + 1) * ROWS] * (1.0 / math.sqrt(SW))).astype(bf16)

    def give_back(r, low=1, high=DP):
        send_blocks(g_send, g_got, g_send_sem, g_got_sem, r, low, high)

    def for_scores(n):
        half = lax.rem(n // BLOCKS, 2)
        return (t_left.at[half], t_right.at[half], s_left.at[half], s_right.at[half]), lax.rem(n, BLOCKS)

    def for_grads(n):
        half = lax.rem(n // BLOCKS, 2)
        return (s_feat.at[half], total.at[half]), lax.rem(n, BLOCKS)

    work = (t_raw, s_raw, t_exp, s_exp, t_top, gain, kl)

    for copy in loads(0):
        copy.wait()
    pack(0, 0)
    pl.semaphore_wait(barrier, DP - 1 + TENSOR - 1)
    send_half(0, 0)
    pack(0, 1)
    send_half(0, 1)
    for r in range(1, RELATIONS):
        for copy in loads(r):
            copy.wait()
        for s in range(SEQS):
            pack(r, s)
            if r == 1:
                send_half(r, s)
    kl[...] = jnp.zeros_like(kl)
    gain[...] = jnp.zeros_like(gain)
    t_exp[...] = jnp.zeros_like(t_exp)
    s_exp[...] = jnp.zeros_like(s_exp)
    s_feat[1] = jnp.zeros_like(s_feat[1])
    total[...] = jnp.zeros_like(total)
    receive(0)
    pipeline_step(for_scores(0), False, None, work)

    def step(n, carry):
        block = lax.rem(n, BLOCKS)
        r = n // BLOCKS

        @pl.when(n == 0)
        def _():
            send_blocks(send, got, send_sem, got_sem, 2)

        @pl.when((block == BLOCKS - 1) & (r < RELATIONS - 1))
        def _():
            receive(r + 1)

        pipeline_step(for_scores(n + 1), True, for_grads(n + 2 * BLOCKS - 1), work)

        @pl.when((block == 0) & (r > 0))
        def _():
            round_grads(r - 1)
            give_back(r - 1)

        @pl.when((block == 0) & (r < RELATIONS - 1))
        def _():
            half = lax.rem(r + 1, 2)
            total[half] = jnp.zeros((SW, LENGTH), f32)

        return carry

    lax.fori_loop(0, RELATIONS * BLOCKS - 1, step, 0)
    pipeline_step(None, True, for_grads(RELATIONS * BLOCKS - 2), work)

    def share(buffer, axis, here, size, which, value):
        buffer[here] = value

        def one(n, carry):
            to = lax.rem(here + n, size)
            pltpu.make_async_remote_copy(
                src_ref=buffer.at[here],
                dst_ref=buffer.at[here],
                send_sem=loss_send_sem.at[which],
                recv_sem=loss_got_sem.at[which],
                device_id={axis: to},
                device_id_type=MESH,
            ).start()
            return carry

        lax.fori_loop(1, size, one, 0)

    def collect(buffer, size, which):
        span = buffer.at[pl.ds(0, size - 1)]
        pltpu.make_async_copy(span, span, loss_got_sem.at[which]).wait()
        return functools.reduce(lambda a, b: a + b, [buffer[n] for n in range(size)])

    part = jnp.broadcast_to(jnp.sum(kl[...], axis=1, keepdims=True), (8, 128))
    share(loss_a, "dp", me, DP, 0, part)
    pipeline_step(None, False, for_grads(RELATIONS * BLOCKS - 1), work)
    round_grads(RELATIONS - 1)
    give_back(RELATIONS - 1, 1, DP // 2)
    share(loss_b, "tensor", lane, TENSOR, 1, collect(loss_a, DP, 0))
    give_back(RELATIONS - 1, DP // 2, DP)
    for r in range(RELATIONS - 1):
        place(r)
    loss_out[...] = collect(loss_b, TENSOR, 1) * (1.0 / (RELATIONS * SEQS * RH * LENGTH))
    for r in range(RELATIONS):
        wait_blocks(send, send_sem, r)
        wait_blocks(g_send, g_send_sem, r)
    for which, buffer, size in ((0, loss_a, DP), (1, loss_b, TENSOR)):
        span = buffer.at[pl.ds(0, size - 1)]
        pltpu.make_async_copy(span, span, loss_send_sem.at[which]).wait()
    place(RELATIONS - 1)


def per_device(teacher_states, student_states):
    dma = pltpu.SemaphoreType.DMA
    loss, grads = pl.pallas_call(
        kernel,
        out_shape=(
            jax.ShapeDtypeStruct((8, 128), f32),
            jax.ShapeDtypeStruct(student_states.shape, bf16),
        ),
        in_specs=[pl.BlockSpec(memory_space=pl.ANY)] * 2,
        out_specs=(pl.BlockSpec(memory_space=pltpu.VMEM), pl.BlockSpec(memory_space=pltpu.VMEM)),
        scratch_shapes=[
            pltpu.VMEM((RELATIONS, ROWS, SEQS, HEADS * TW), bf16),
            pltpu.VMEM((RELATIONS, ROWS, SEQS, HEADS * SW), bf16),
            pltpu.VMEM((RELATIONS, DP, SW + ROWS, 128), bf16),
            pltpu.VMEM((RELATIONS, DP, SW + ROWS, 128), bf16),
            pltpu.VMEM((RELATIONS, DP, SW, ROWS), bf16),
            pltpu.VMEM((RELATIONS, DP, SW, ROWS), bf16),
            pltpu.VMEM((2, LENGTH, 2 * TW), bf16),
            pltpu.VMEM((2, LENGTH, 2 * TW), bf16),
            pltpu.VMEM((2, LENGTH, 128), bf16),
            pltpu.VMEM((2, 128, LENGTH), bf16),
            pltpu.VMEM((2, SW, LENGTH), bf16),
            pltpu.VMEM((2, SW, LENGTH), f32),
            pltpu.VMEM((LENGTH, BLOCK), f32),
            pltpu.VMEM((LENGTH, BLOCK), f32),
            pltpu.VMEM((LENGTH, BLOCK), f32),
            pltpu.VMEM((LENGTH, BLOCK), f32),
            pltpu.VMEM((8 * COUNT, BLOCK), f32),
            pltpu.VMEM((8 * (COUNT + 1), BLOCK), f32),
            pltpu.VMEM((1, BLOCK), f32),
            pltpu.VMEM((DP, 8, 128), f32),
            pltpu.VMEM((TENSOR, 8, 128), f32),
            dma((2, RELATIONS)),
            dma((RELATIONS,)),
            dma((RELATIONS,)),
            dma((RELATIONS,)),
            dma((RELATIONS,)),
            dma((2,)),
            dma((2,)),
        ],
        compiler_params=pltpu.CompilerParams(
            collective_id=0, has_side_effects=True, vmem_limit_bytes=54400 * 1024
        ),
    )(teacher_states, student_states)
    return loss[0, 0], grads


def solution(mesh):
    placed = (P(None, "dp", None, "tensor"), P(None, "dp", None, "tensor"))
    return jax.shard_map(
        per_device,
        mesh=mesh,
        in_specs=placed,
        out_specs=(P(), P(None, "dp", None, "tensor")),
        check_vma=False,
    )
```

```python
import functools
import math

import jax
import jax.numpy as jnp
from jax import lax
from jax.experimental import pallas as pl
from jax.experimental.pallas import tpu as pltpu
from jax.sharding import PartitionSpec as P

RELATIONS = 3
SEQS = 2
RH = 64
LENGTH = 2048
TW = 128
SW = 48
DP = 16
TENSOR = 8
ROWS = LENGTH // DP
HEADS = RH // TENSOR
BLOCK = 256
BLOCKS = LENGTH // BLOCK
CHUNK = 512
COUNT = LENGTH // CHUNK
PIECE = 32
LOSS_SCALE = 16.0
LOG2E = 1.0 / math.log(2.0)
T_SCALE = LOG2E / math.sqrt(TW)
S_SCALE = LOG2E / math.sqrt(SW)
MESH = pl.DeviceIdType.MESH
f32 = jnp.float32
bf16 = jnp.bfloat16


def dot_nt(a, b):
    return lax.dot_general(a, b, (((1,), (1,)), ((), ())), preferred_element_type=f32)


def dot_nn(a, b):
    return jnp.dot(a, b, preferred_element_type=f32)


def prepare(blocks, t_left, t_right, s_left, s_right, s_feat):
    norms = []
    largest = jnp.zeros((1, ROWS), f32)
    for p in range(DP):
        x = blocks[p, 0:SW, :].astype(f32)
        square = jnp.sum(x * x, axis=0, keepdims=True)
        norms.append(square)
        largest = jnp.maximum(largest, square)
    largest = jnp.max(largest, axis=1, keepdims=True)
    first = lax.broadcasted_iota(jnp.int32, (16, ROWS), 0) == 0
    ones = jnp.where(first, 1.0, 0.0)
    zeros = jnp.zeros((16, ROWS), f32)
    for p in range(DP):
        rows = slice(p * ROWS, (p + 1) * ROWS)
        features = blocks[p, 0:SW, :]
        x = features.astype(f32)
        scaled = x * S_SCALE
        high = scaled.astype(bf16)
        low = (scaled - high.astype(f32)).astype(bf16)
        shift = (0.5 * S_SCALE) * (jnp.sqrt(norms[p] * largest) + norms[p])
        shift = jnp.where(first, -shift, 0.0).astype(bf16)
        s_right[:, rows] = jnp.concatenate([high, low, shift, zeros.astype(bf16)], axis=0)
        s_left[rows, :] = jnp.concatenate([x, x, ones, zeros], axis=0).T.astype(bf16)
        s_feat[:, rows] = features
        x = blocks[p, SW:, :]
        scaled = x.astype(f32) * T_SCALE
        high = scaled.astype(bf16)
        t_left[rows, 0:TW] = x
        t_left[rows, TW:] = x
        t_right[rows, 0:TW] = high
        t_right[rows, TW:] = (scaled - high.astype(f32)).astype(bf16)


def fold(x, op):
    parts = [x[8 * n : 8 * n + 8, :] for n in range(x.shape[0] // 8)]
    while len(parts) > 1:
        parts = [op(*parts[n : n + 2]) if n + 1 < len(parts) else parts[n] for n in range(0, len(parts), 2)]
    return parts[0]


def pipeline_step(scores, exps, grads, work):
    t_raw, s_raw, t_exp, s_exp, t_top, gain, kl = work
    repeat = PIECE // 8
    if grads is not None:
        (s_feat, total), block = grads
        last = pl.ds(pl.multiple_of(block * BLOCK, BLOCK), BLOCK)
        x_last = s_feat[:, last]
        s_gain = jnp.concatenate([gain[COUNT * 8 :, :]] * repeat, axis=0)
        t_gain = [gain[k * 8 : k * 8 + 8, :] for k in range(COUNT)]
        forward = jnp.zeros((SW, BLOCK), f32)
    if exps:
        t_max = [t_top[k * 8 : k * 8 + 8, :] for k in range(COUNT)]
        t_sum, cross = [], []
        s_sum = jnp.zeros((8, BLOCK), f32)
    if scores is not None:
        (t_left, t_right, s_left, s_right), block = scores
        own = pl.ds(pl.multiple_of(block * BLOCK, BLOCK), BLOCK)
        t_own = t_right[own, :]
        s_own = s_right[:, own]
    for k in range(COUNT):
        part = slice(k * CHUNK, (k + 1) * CHUNK)
        pieces = [slice(n, n + PIECE) for n in range(k * CHUNK, (k + 1) * CHUNK, PIECE)]
        if grads is not None:
            t_wide = jnp.concatenate([t_gain[k]] * repeat, axis=0)
            grad = jnp.concatenate(
                [(s_exp[n, :] * s_gain - t_exp[n, :] * t_wide).astype(bf16) for n in pieces], axis=0
            )
            forward = forward + dot_nn(s_feat[:, part], grad)
            total[:, part] += dot_nt(x_last, grad)
        if exps:
            top_wide = jnp.concatenate([t_max[k]] * repeat, axis=0)
            z = jnp.zeros((8, BLOCK), f32)
            c = jnp.zeros((8, BLOCK), f32)
            for n in pieces:
                t = t_raw[n, :] - top_wide
                s = s_raw[n, :]
                te = jnp.exp2(t)
                se = jnp.exp2(s)
                z = z + fold(te, jnp.add)
                s_sum = s_sum + fold(se, jnp.add)
                c = c + fold(te * (t - s), jnp.add)
                t_exp[n, :] = te
                s_exp[n, :] = se
            t_sum.append(z)
            cross.append(c)
        if scores is not None:
            t_all = dot_nt(t_left[part, :], t_own)
            t_raw[part, :] = t_all
            t_top[k * 8 : k * 8 + 8, :] = fold(t_all, jnp.maximum)
            s_raw[part, :] = dot_nn(s_left[part, :], s_own)
    if grads is not None:
        total[:, last] += forward
    if exps:
        top = functools.reduce(jnp.maximum, t_max)
        top = jnp.broadcast_to(jnp.max(top, axis=0, keepdims=True), (8, BLOCK))
        lift = [jnp.exp2(x - top) for x in t_max]
        z = sum(f * x for f, x in zip(lift, t_sum))
        c = sum(f * (c + (m - top) * x) for f, c, m, x in zip(lift, cross, t_max, t_sum))
        z = jnp.sum(z, axis=0, keepdims=True)
        c = jnp.sum(c, axis=0, keepdims=True)
        s_sum = jnp.sum(s_sum, axis=0, keepdims=True)
        kl[...] += math.log(2.0) * c / z - jnp.log(z) + jnp.log(s_sum)
        t_gain = jnp.broadcast_to(LOSS_SCALE / z, (8, BLOCK))
        for k in range(COUNT):
            gain[k * 8 : k * 8 + 8, :] = t_gain * lift[k]
        gain[COUNT * 8 :, :] = jnp.broadcast_to(LOSS_SCALE / s_sum, (8, BLOCK))


def kernel(
    teacher_hbm, student_hbm, loss_out, grads_out,
    t_in, s_in, send, got, g_send, g_got,
    t_left, t_right, s_left, s_right, s_feat, total,
    t_raw, s_raw, t_exp, s_exp, t_top, gain, kl,
    loss_a, loss_b,
    load_sem, send_sem, got_sem, g_send_sem, g_got_sem, loss_send_sem, loss_got_sem,
):
    me = lax.axis_index("dp")
    lane = lax.axis_index("tensor")

    def loads(r):
        return (
            pltpu.make_async_copy(student_hbm.at[r], s_in.at[r], load_sem.at[1, r]),
            pltpu.make_async_copy(teacher_hbm.at[r], t_in.at[r], load_sem.at[0, r]),
        )

    for r in range(RELATIONS):
        for copy in loads(r):
            copy.start()

    barrier = pltpu.get_barrier_semaphore()

    def greet_dp(n, carry):
        pl.semaphore_signal(barrier, inc=1, device_id={"dp": lax.rem(me + n, DP)}, device_id_type=MESH)
        return carry

    def greet_tensor(n, carry):
        pl.semaphore_signal(barrier, inc=1, device_id={"tensor": lax.rem(lane + n, TENSOR)}, device_id_type=MESH)
        return carry

    lax.fori_loop(1, DP, greet_dp, 0)
    lax.fori_loop(1, TENSOR, greet_tensor, 0)

    def pack(r, s):
        x = s_in[r, :, s, :].astype(f32).T.astype(bf16)
        for a in range(HEADS):
            send[r, SEQS * a + s, 0:SW, :] = x[a * SW : (a + 1) * SW, :]
        x = t_in[r, :, s, :]
        for a in range(HEADS):
            send[r, SEQS * a + s, SW:, :] = x[:, a * TW : (a + 1) * TW]

    def send_one(source, target, source_sem, target_sem, r, to):
        pltpu.make_async_remote_copy(
            src_ref=source.at[r, to],
            dst_ref=target.at[r, me],
            send_sem=source_sem.at[r],
            recv_sem=target_sem.at[r],
            device_id={"dp": to},
            device_id_type=MESH,
        ).start()

    def send_blocks(source, target, source_sem, target_sem, r, low=1, high=DP):
        def one(n, carry):
            send_one(source, target, source_sem, target_sem, r, lax.rem(me + n, DP))
            return carry

        lax.fori_loop(low, high, one, 0)

    def send_half(r, s):
        odd = lax.rem(me + s, SEQS)

        def one(n, carry):
            send_one(send, got, send_sem, got_sem, r, lax.rem(me + odd + SEQS * n, DP))
            return carry

        lax.fori_loop(1 - odd, HEADS, one, 0)

    def wait_blocks(buffer, sem, r):
        span = buffer.at[r, pl.ds(0, DP - 1)]
        pltpu.make_async_copy(span, span, sem.at[r]).wait()

    def place(r):
        g_got[r, me] = g_send[r, me]
        wait_blocks(g_got, g_got_sem, r)
        for s in range(SEQS):
            x = jnp.concatenate([g_got[r, SEQS * a + s] for a in range(HEADS)], axis=0)
            grads_out[r, :, s, :] = x.T

    def receive(r):
        got[r, me] = send[r, me]
        wait_blocks(got, got_sem, r)
        half = lax.rem(r, 2)
        prepare(got.at[r], t_left.at[half], t_right.at[half], s_left.at[half], s_right.at[half], s_feat.at[half])

    def round_grads(r):
        half = lax.rem(r, 2)
        for p in range(DP):
            g_send[r, p] = (total[half, :, p * ROWS : (p + 1) * ROWS] * (1.0 / math.sqrt(SW))).astype(bf16)

    def give_back(r, low=1, high=DP):
        send_blocks(g_send, g_got, g_send_sem, g_got_sem, r, low, high)

    def for_scores(n):
        half = lax.rem(n // BLOCKS, 2)
        return (t_left.at[half], t_right.at[half], s_left.at[half], s_right.at[half]), lax.rem(n, BLOCKS)

    def for_grads(n):
        half = lax.rem(n // BLOCKS, 2)
        return (s_feat.at[half], total.at[half]), lax.rem(n, BLOCKS)

    work = (t_raw, s_raw, t_exp, s_exp, t_top, gain, kl)

    for copy in loads(0):
        copy.wait()
    pack(0, 0)
    pl.semaphore_wait(barrier, DP - 1 + TENSOR - 1)
    send_half(0, 0)
    pack(0, 1)
    send_half(0, 1)
    for r in range(1, RELATIONS):
        for copy in loads(r):
            copy.wait()
        for s in range(SEQS):
            pack(r, s)
            send_half(r, s)
    kl[...] = jnp.zeros_like(kl)
    gain[...] = jnp.zeros_like(gain)
    t_exp[...] = jnp.zeros_like(t_exp)
    s_exp[...] = jnp.zeros_like(s_exp)
    s_feat[1] = jnp.zeros_like(s_feat[1])
    total[...] = jnp.zeros_like(total)
    receive(0)
    pipeline_step(for_scores(0), False, None, work)

    def step(n, carry):
        block = lax.rem(n, BLOCKS)
        r = n // BLOCKS

        @pl.when((block == BLOCKS - 1) & (r < RELATIONS - 1))
        def _():
            receive(r + 1)

        pipeline_step(for_scores(n + 1), True, for_grads(n + 2 * BLOCKS - 1), work)

        @pl.when((block == 0) & (r > 0))
        def _():
            round_grads(r - 1)
            give_back(r - 1)

        @pl.when((block == 0) & (r < RELATIONS - 1))
        def _():
            half = lax.rem(r + 1, 2)
            total[half] = jnp.zeros((SW, LENGTH), f32)

        return carry

    lax.fori_loop(0, RELATIONS * BLOCKS - 1, step, 0)
    pipeline_step(None, True, for_grads(RELATIONS * BLOCKS - 2), work)

    def share(buffer, axis, here, size, which, value):
        buffer[here] = value

        def one(n, carry):
            to = lax.rem(here + n, size)
            pltpu.make_async_remote_copy(
                src_ref=buffer.at[here],
                dst_ref=buffer.at[here],
                send_sem=loss_send_sem.at[which],
                recv_sem=loss_got_sem.at[which],
                device_id={axis: to},
                device_id_type=MESH,
            ).start()
            return carry

        lax.fori_loop(1, size, one, 0)

    def collect(buffer, size, which):
        span = buffer.at[pl.ds(0, size - 1)]
        pltpu.make_async_copy(span, span, loss_got_sem.at[which]).wait()
        return functools.reduce(lambda a, b: a + b, [buffer[n] for n in range(size)])

    part = jnp.broadcast_to(jnp.sum(kl[...], axis=1, keepdims=True), (8, 128))
    share(loss_a, "dp", me, DP, 0, part)
    pipeline_step(None, False, for_grads(RELATIONS * BLOCKS - 1), work)
    round_grads(RELATIONS - 1)
    give_back(RELATIONS - 1, 1, DP // 2)
    share(loss_b, "tensor", lane, TENSOR, 1, collect(loss_a, DP, 0))
    give_back(RELATIONS - 1, DP // 2, DP)
    for r in range(RELATIONS - 1):
        place(r)
    loss_out[...] = collect(loss_b, TENSOR, 1) * (1.0 / (RELATIONS * SEQS * RH * LENGTH))
    for r in range(RELATIONS):
        wait_blocks(send, send_sem, r)
        wait_blocks(g_send, g_send_sem, r)
    for which, buffer, size in ((0, loss_a, DP), (1, loss_b, TENSOR)):
        span = buffer.at[pl.ds(0, size - 1)]
        pltpu.make_async_copy(span, span, loss_send_sem.at[which]).wait()
    place(RELATIONS - 1)


def per_device(teacher_states, student_states):
    dma = pltpu.SemaphoreType.DMA
    loss, grads = pl.pallas_call(
        kernel,
        out_shape=(
            jax.ShapeDtypeStruct((8, 128), f32),
            jax.ShapeDtypeStruct(student_states.shape, bf16),
        ),
        in_specs=[pl.BlockSpec(memory_space=pl.ANY)] * 2,
        out_specs=(pl.BlockSpec(memory_space=pltpu.VMEM), pl.BlockSpec(memory_space=pltpu.VMEM)),
        scratch_shapes=[
            pltpu.VMEM((RELATIONS, ROWS, SEQS, HEADS * TW), bf16),
            pltpu.VMEM((RELATIONS, ROWS, SEQS, HEADS * SW), bf16),
            pltpu.VMEM((RELATIONS, DP, SW + ROWS, 128), bf16),
            pltpu.VMEM((RELATIONS, DP, SW + ROWS, 128), bf16),
            pltpu.VMEM((RELATIONS, DP, SW, ROWS), bf16),
            pltpu.VMEM((RELATIONS, DP, SW, ROWS), bf16),
            pltpu.VMEM((2, LENGTH, 2 * TW), bf16),
            pltpu.VMEM((2, LENGTH, 2 * TW), bf16),
            pltpu.VMEM((2, LENGTH, 128), bf16),
            pltpu.VMEM((2, 128, LENGTH), bf16),
            pltpu.VMEM((2, SW, LENGTH), bf16),
            pltpu.VMEM((2, SW, LENGTH), f32),
            pltpu.VMEM((LENGTH, BLOCK), f32),
            pltpu.VMEM((LENGTH, BLOCK), f32),
            pltpu.VMEM((LENGTH, BLOCK), f32),
            pltpu.VMEM((LENGTH, BLOCK), f32),
            pltpu.VMEM((8 * COUNT, BLOCK), f32),
            pltpu.VMEM((8 * (COUNT + 1), BLOCK), f32),
            pltpu.VMEM((1, BLOCK), f32),
            pltpu.VMEM((DP, 8, 128), f32),
            pltpu.VMEM((TENSOR, 8, 128), f32),
            dma((2, RELATIONS)),
            dma((RELATIONS,)),
            dma((RELATIONS,)),
            dma((RELATIONS,)),
            dma((RELATIONS,)),
            dma((2,)),
            dma((2,)),
        ],
        compiler_params=pltpu.CompilerParams(
            collective_id=0, has_side_effects=True, vmem_limit_bytes=54400 * 1024
        ),
    )(teacher_states, student_states)
    return loss[0, 0], grads


def solution(mesh):
    placed = (P(None, "dp", None, "tensor"), P(None, "dp", None, "tensor"))
    return jax.shard_map(
        per_device,
        mesh=mesh,
        in_specs=placed,
        out_specs=(P(), P(None, "dp", None, "tensor")),
        check_vma=False,
    )
```

```python
import functools
import math

import jax
import jax.numpy as jnp
from jax import lax
from jax.experimental import pallas as pl
from jax.experimental.pallas import tpu as pltpu
from jax.sharding import PartitionSpec as P

RELATIONS = 3
SEQS = 2
RH = 64
LENGTH = 2048
TW = 128
SW = 48
DP = 16
TENSOR = 8
ROWS = LENGTH // DP
HEADS = RH // TENSOR
BLOCK = 256
BLOCKS = LENGTH // BLOCK
CHUNK = 512
COUNT = LENGTH // CHUNK
PIECE = 16
LOSS_SCALE = 16.0
LOG2E = 1.0 / math.log(2.0)
T_SCALE = LOG2E / math.sqrt(TW)
S_SCALE = LOG2E / math.sqrt(SW)
MESH = pl.DeviceIdType.MESH
f32 = jnp.float32
bf16 = jnp.bfloat16


def dot_nt(a, b):
    return lax.dot_general(a, b, (((1,), (1,)), ((), ())), preferred_element_type=f32)


def dot_nn(a, b):
    return jnp.dot(a, b, preferred_element_type=f32)


def prepare(blocks, t_left, t_right, s_left, s_right, s_feat):
    norms = []
    largest = jnp.zeros((1, ROWS), f32)
    for p in range(DP):
        x = blocks[p, 0:SW, :].astype(f32)
        square = jnp.sum(x * x, axis=0, keepdims=True)
        norms.append(square)
        largest = jnp.maximum(largest, square)
    largest = jnp.max(largest, axis=1, keepdims=True)
    first = lax.broadcasted_iota(jnp.int32, (16, ROWS), 0) == 0
    ones = jnp.where(first, 1.0, 0.0)
    zeros = jnp.zeros((16, ROWS), f32)
    for p in range(DP):
        rows = slice(p * ROWS, (p + 1) * ROWS)
        features = blocks[p, 0:SW, :]
        x = features.astype(f32)
        scaled = x * S_SCALE
        high = scaled.astype(bf16)
        low = (scaled - high.astype(f32)).astype(bf16)
        shift = (0.5 * S_SCALE) * (jnp.sqrt(norms[p] * largest) + norms[p])
        shift = jnp.where(first, -shift, 0.0).astype(bf16)
        s_right[:, rows] = jnp.concatenate([high, low, shift, zeros.astype(bf16)], axis=0)
        s_left[rows, :] = jnp.concatenate([x, x, ones, zeros], axis=0).T.astype(bf16)
        s_feat[:, rows] = features
        x = blocks[p, SW:, :]
        scaled = x.astype(f32) * T_SCALE
        high = scaled.astype(bf16)
        t_left[rows, 0:TW] = x
        t_left[rows, TW:] = x
        t_right[rows, 0:TW] = high
        t_right[rows, TW:] = (scaled - high.astype(f32)).astype(bf16)


def fold(x, op):
    parts = [x[8 * n : 8 * n + 8, :] for n in range(x.shape[0] // 8)]
    while len(parts) > 1:
        parts = [op(*parts[n : n + 2]) if n + 1 < len(parts) else parts[n] for n in range(0, len(parts), 2)]
    return parts[0]


def pipeline_step(scores, exps, grads, work):
    t_raw, s_raw, t_exp, s_exp, t_top, gain, kl = work
    repeat = PIECE // 8
    if grads is not None:
        (s_feat, total), block = grads
        last = pl.ds(pl.multiple_of(block * BLOCK, BLOCK), BLOCK)
        x_last = s_feat[:, last]
        s_gain = jnp.concatenate([gain[COUNT * 8 :, :]] * repeat, axis=0)
        t_gain = [gain[k * 8 : k * 8 + 8, :] for k in range(COUNT)]
        forward = jnp.zeros((SW, BLOCK), f32)
    if exps:
        t_max = [t_top[k * 8 : k * 8 + 8, :] for k in range(COUNT)]
        t_sum, cross = [], []
        s_sum = jnp.zeros((8, BLOCK), f32)
    if scores is not None:
        (t_left, t_right, s_left, s_right), block = scores
        own = pl.ds(pl.multiple_of(block * BLOCK, BLOCK), BLOCK)
        t_own = t_right[own, :]
        s_own = s_right[:, own]
    for k in range(COUNT):
        part = slice(k * CHUNK, (k + 1) * CHUNK)
        pieces = [slice(n, n + PIECE) for n in range(k * CHUNK, (k + 1) * CHUNK, PIECE)]
        if grads is not None:
            t_wide = jnp.concatenate([t_gain[k]] * repeat, axis=0)
            grad = jnp.concatenate(
                [(s_exp[n, :] * s_gain - t_exp[n, :] * t_wide).astype(bf16) for n in pieces], axis=0
            )
            forward = forward + dot_nn(s_feat[:, part], grad)
            total[:, part] += dot_nt(x_last, grad)
        if exps:
            top_wide = jnp.concatenate([t_max[k]] * repeat, axis=0)
            z = jnp.zeros((8, BLOCK), f32)
            c = jnp.zeros((8, BLOCK), f32)
            for n in pieces:
                t = t_raw[n, :] - top_wide
                s = s_raw[n, :]
                te = jnp.exp2(t)
                se = jnp.exp2(s)
                z = z + fold(te, jnp.add)
                s_sum = s_sum + fold(se, jnp.add)
                c = c + fold(te * (t - s), jnp.add)
                t_exp[n, :] = te
                s_exp[n, :] = se
            t_sum.append(z)
            cross.append(c)
        if scores is not None:
            t_all = dot_nt(t_left[part, :], t_own)
            t_raw[part, :] = t_all
            t_top[k * 8 : k * 8 + 8, :] = fold(t_all, jnp.maximum)
            s_raw[part, :] = dot_nn(s_left[part, :], s_own)
    if grads is not None:
        total[:, last] += forward
    if exps:
        top = functools.reduce(jnp.maximum, t_max)
        top = jnp.broadcast_to(jnp.max(top, axis=0, keepdims=True), (8, BLOCK))
        lift = [jnp.exp2(x - top) for x in t_max]
        z = sum(f * x for f, x in zip(lift, t_sum))
        c = sum(f * (c + (m - top) * x) for f, c, m, x in zip(lift, cross, t_max, t_sum))
        z = jnp.sum(z, axis=0, keepdims=True)
        c = jnp.sum(c, axis=0, keepdims=True)
        s_sum = jnp.sum(s_sum, axis=0, keepdims=True)
        kl[...] += math.log(2.0) * c / z - jnp.log(z) + jnp.log(s_sum)
        t_gain = jnp.broadcast_to(LOSS_SCALE / z, (8, BLOCK))
        for k in range(COUNT):
            gain[k * 8 : k * 8 + 8, :] = t_gain * lift[k]
        gain[COUNT * 8 :, :] = jnp.broadcast_to(LOSS_SCALE / s_sum, (8, BLOCK))


def kernel(
    teacher_hbm, student_hbm, loss_out, grads_out,
    t_in, s_in, send, got, g_send, g_got,
    t_left, t_right, s_left, s_right, s_feat, total,
    t_raw, s_raw, t_exp, s_exp, t_top, gain, kl,
    loss_a, loss_b,
    load_sem, send_sem, got_sem, g_send_sem, g_got_sem, loss_send_sem, loss_got_sem,
):
    me = lax.axis_index("dp")
    lane = lax.axis_index("tensor")

    def loads(r):
        return (
            pltpu.make_async_copy(student_hbm.at[r], s_in.at[r], load_sem.at[1, r]),
            pltpu.make_async_copy(teacher_hbm.at[r], t_in.at[r], load_sem.at[0, r]),
        )

    for r in range(RELATIONS):
        for copy in loads(r):
            copy.start()

    barrier = pltpu.get_barrier_semaphore()

    def greet_dp(n, carry):
        pl.semaphore_signal(barrier, inc=1, device_id={"dp": lax.rem(me + n, DP)}, device_id_type=MESH)
        return carry

    def greet_tensor(n, carry):
        pl.semaphore_signal(barrier, inc=1, device_id={"tensor": lax.rem(lane + n, TENSOR)}, device_id_type=MESH)
        return carry

    lax.fori_loop(1, DP, greet_dp, 0)
    lax.fori_loop(1, TENSOR, greet_tensor, 0)

    def pack(r, s):
        x = s_in[r, :, s, :].astype(f32).T.astype(bf16)
        for a in range(HEADS):
            send[r, SEQS * a + s, 0:SW, :] = x[a * SW : (a + 1) * SW, :]
        x = t_in[r, :, s, :]
        for a in range(HEADS):
            send[r, SEQS * a + s, SW:, :] = x[:, a * TW : (a + 1) * TW]

    def send_one(source, target, source_sem, target_sem, r, to):
        pltpu.make_async_remote_copy(
            src_ref=source.at[r, to],
            dst_ref=target.at[r, me],
            send_sem=source_sem.at[r],
            recv_sem=target_sem.at[r],
            device_id={"dp": to},
            device_id_type=MESH,
        ).start()

    def send_blocks(source, target, source_sem, target_sem, r, low=1, high=DP):
        def one(n, carry):
            send_one(source, target, source_sem, target_sem, r, lax.rem(me + n, DP))
            return carry

        lax.fori_loop(low, high, one, 0)

    def send_half(r, s):
        odd = lax.rem(me + s, SEQS)

        def one(n, carry):
            send_one(send, got, send_sem, got_sem, r, lax.rem(me + odd + SEQS * n, DP))
            return carry

        lax.fori_loop(1 - odd, HEADS, one, 0)

    def wait_blocks(buffer, sem, r):
        span = buffer.at[r, pl.ds(0, DP - 1)]
        pltpu.make_async_copy(span, span, sem.at[r]).wait()

    def place(r):
        g_got[r, me] = g_send[r, me]
        wait_blocks(g_got, g_got_sem, r)
        for s in range(SEQS):
            x = jnp.concatenate([g_got[r, SEQS * a + s] for a in range(HEADS)], axis=0)
            grads_out[r, :, s, :] = x.T

    def receive(r):
        got[r, me] = send[r, me]
        wait_blocks(got, got_sem, r)
        half = lax.rem(r, 2)
        prepare(got.at[r], t_left.at[half], t_right.at[half], s_left.at[half], s_right.at[half], s_feat.at[half])

    def round_grads(r):
        half = lax.rem(r, 2)
        for p in range(DP):
            g_send[r, p] = (total[half, :, p * ROWS : (p + 1) * ROWS] * (1.0 / math.sqrt(SW))).astype(bf16)

    def give_back(r, low=1, high=DP):
        send_blocks(g_send, g_got, g_send_sem, g_got_sem, r, low, high)

    def for_scores(n):
        half = lax.rem(n // BLOCKS, 2)
        return (t_left.at[half], t_right.at[half], s_left.at[half], s_right.at[half]), lax.rem(n, BLOCKS)

    def for_grads(n):
        half = lax.rem(n // BLOCKS, 2)
        return (s_feat.at[half], total.at[half]), lax.rem(n, BLOCKS)

    work = (t_raw, s_raw, t_exp, s_exp, t_top, gain, kl)

    for copy in loads(0):
        copy.wait()
    pack(0, 0)
    pl.semaphore_wait(barrier, DP - 1 + TENSOR - 1)
    send_half(0, 0)
    pack(0, 1)
    send_half(0, 1)
    for r in range(1, RELATIONS):
        for copy in loads(r):
            copy.wait()
        for s in range(SEQS):
            pack(r, s)
            send_half(r, s)
    kl[...] = jnp.zeros_like(kl)
    gain[...] = jnp.zeros_like(gain)
    t_exp[...] = jnp.zeros_like(t_exp)
    s_exp[...] = jnp.zeros_like(s_exp)
    s_feat[1] = jnp.zeros_like(s_feat[1])
    total[...] = jnp.zeros_like(total)
    receive(0)
    pipeline_step(for_scores(0), False, None, work)

    def step(n, carry):
        block = lax.rem(n, BLOCKS)
        r = n // BLOCKS

        @pl.when((block == BLOCKS - 1) & (r < RELATIONS - 1))
        def _():
            receive(r + 1)

        pipeline_step(for_scores(n + 1), True, for_grads(n + 2 * BLOCKS - 1), work)

        @pl.when((block == 0) & (r > 0))
        def _():
            round_grads(r - 1)
            give_back(r - 1)

        @pl.when((block == 0) & (r < RELATIONS - 1))
        def _():
            half = lax.rem(r + 1, 2)
            total[half] = jnp.zeros((SW, LENGTH), f32)

        return carry

    lax.fori_loop(0, RELATIONS * BLOCKS - 1, step, 0)
    pipeline_step(None, True, for_grads(RELATIONS * BLOCKS - 2), work)

    def share(buffer, axis, here, size, which, value):
        buffer[here] = value

        def one(n, carry):
            to = lax.rem(here + n, size)
            pltpu.make_async_remote_copy(
                src_ref=buffer.at[here],
                dst_ref=buffer.at[here],
                send_sem=loss_send_sem.at[which],
                recv_sem=loss_got_sem.at[which],
                device_id={axis: to},
                device_id_type=MESH,
            ).start()
            return carry

        lax.fori_loop(1, size, one, 0)

    def collect(buffer, size, which):
        span = buffer.at[pl.ds(0, size - 1)]
        pltpu.make_async_copy(span, span, loss_got_sem.at[which]).wait()
        return functools.reduce(lambda a, b: a + b, [buffer[n] for n in range(size)])

    part = jnp.broadcast_to(jnp.sum(kl[...], axis=1, keepdims=True), (8, 128))
    share(loss_a, "dp", me, DP, 0, part)
    pipeline_step(None, False, for_grads(RELATIONS * BLOCKS - 1), work)
    round_grads(RELATIONS - 1)
    give_back(RELATIONS - 1, 1, DP // 2)
    share(loss_b, "tensor", lane, TENSOR, 1, collect(loss_a, DP, 0))
    give_back(RELATIONS - 1, DP // 2, DP)
    for r in range(RELATIONS - 1):
        place(r)
    loss_out[...] = collect(loss_b, TENSOR, 1) * (1.0 / (RELATIONS * SEQS * RH * LENGTH))
    place(RELATIONS - 1)
    for r in range(RELATIONS):
        wait_blocks(send, send_sem, r)
        wait_blocks(g_send, g_send_sem, r)
    for which, buffer, size in ((0, loss_a, DP), (1, loss_b, TENSOR)):
        span = buffer.at[pl.ds(0, size - 1)]
        pltpu.make_async_copy(span, span, loss_send_sem.at[which]).wait()


def per_device(teacher_states, student_states):
    dma = pltpu.SemaphoreType.DMA
    loss, grads = pl.pallas_call(
        kernel,
        out_shape=(
            jax.ShapeDtypeStruct((8, 128), f32),
            jax.ShapeDtypeStruct(student_states.shape, bf16),
        ),
        in_specs=[pl.BlockSpec(memory_space=pl.ANY)] * 2,
        out_specs=(pl.BlockSpec(memory_space=pltpu.VMEM), pl.BlockSpec(memory_space=pltpu.VMEM)),
        scratch_shapes=[
            pltpu.VMEM((RELATIONS, ROWS, SEQS, HEADS * TW), bf16),
            pltpu.VMEM((RELATIONS, ROWS, SEQS, HEADS * SW), bf16),
            pltpu.VMEM((RELATIONS, DP, SW + ROWS, 128), bf16),
            pltpu.VMEM((RELATIONS, DP, SW + ROWS, 128), bf16),
            pltpu.VMEM((RELATIONS, DP, SW, ROWS), bf16),
            pltpu.VMEM((RELATIONS, DP, SW, ROWS), bf16),
            pltpu.VMEM((2, LENGTH, 2 * TW), bf16),
            pltpu.VMEM((2, LENGTH, 2 * TW), bf16),
            pltpu.VMEM((2, LENGTH, 128), bf16),
            pltpu.VMEM((2, 128, LENGTH), bf16),
            pltpu.VMEM((2, SW, LENGTH), bf16),
            pltpu.VMEM((2, SW, LENGTH), f32),
            pltpu.VMEM((LENGTH, BLOCK), f32),
            pltpu.VMEM((LENGTH, BLOCK), f32),
            pltpu.VMEM((LENGTH, BLOCK), f32),
            pltpu.VMEM((LENGTH, BLOCK), f32),
            pltpu.VMEM((8 * COUNT, BLOCK), f32),
            pltpu.VMEM((8 * (COUNT + 1), BLOCK), f32),
            pltpu.VMEM((1, BLOCK), f32),
            pltpu.VMEM((DP, 8, 128), f32),
            pltpu.VMEM((TENSOR, 8, 128), f32),
            dma((2, RELATIONS)),
            dma((RELATIONS,)),
            dma((RELATIONS,)),
            dma((RELATIONS,)),
            dma((RELATIONS,)),
            dma((2,)),
            dma((2,)),
        ],
        compiler_params=pltpu.CompilerParams(
            collective_id=0, has_side_effects=True, vmem_limit_bytes=54400 * 1024
        ),
    )(teacher_states, student_states)
    return loss[0, 0], grads


def solution(mesh):
    placed = (P(None, "dp", None, "tensor"), P(None, "dp", None, "tensor"))
    return jax.shard_map(
        per_device,
        mesh=mesh,
        in_specs=placed,
        out_specs=(P(), P(None, "dp", None, "tensor")),
        check_vma=False,
    )
```
